32 devices in a mesh: groups: 2 (over x), seq: 16 (over z, y, core).
Axes of the slice: x: 2, y: 2, z: 4, core: 2. Of those that a mesh axis runs over, the one named last changes fastest.
Arguments:
- queries: bfloat16 [8192, 4096], P(('groups', 'seq')), parts along dimension 0, may hold values from -12 to 12
- keys: bfloat16 [8192, 512], P(('groups', 'seq')), parts along dimension 0, may hold values from -6 to 6
- values: bfloat16 [8192, 512], P(('groups', 'seq')), parts along dimension 0, may hold values from -6 to 6
- grad_out: bfloat16 [8192, 4096], P(('groups', 'seq')), parts along dimension 0, may hold values from -6 to 6
- episode_lengths: int32 [32], P('groups'), parts along dimension 0, may hold values from 1 to 512, 4096 in all
Outputs:
- attn_out: bfloat16 [8192, 4096], P(('groups', 'seq')), parts along dimension 0
- grad_queries: bfloat16 [8192, 4096], P(('groups', 'seq')), parts along dimension 0
- grad_keys: bfloat16 [8192, 512], P(('groups', 'seq')), parts along dimension 0
- grad_values: bfloat16 [8192, 512], P(('groups', 'seq')), parts along dimension 0
The draws below stay inside these ranges and needn't reach their ends.
There are 2 independent parts, one for each index of `groups`. The reference program is written for one: setup_inputs(seed, part) draws one part's arguments, and reference() takes and returns one part's arrays. A program takes and returns all parts, laid end to end along the dimension named above; each array names one. Nothing has to cross between parts.
Inputs may be any that keep to these rules, and one draw needn't show every extreme that they name: `episode_lengths`: the lengths sum to 4096; the largest is exactly 512.
All inputs are finite; a program needn't handle non-finite values.
Results may differ from the reference program's by a relative error of at most 0.015.
Values may be sent and summed in bfloat16 or wider, within the bound.
No kernel may reach another device: no remote copies, remote signals or barrier semaphores. Data moves between devices by JAX's collectives and lax.ppermute only.
A program may use at most 64 MiB of HBM per device.

```python
import math
import jax
import jax.numpy as jnp
import numpy as np
from jax import lax

HEADS = 32
KV_HEADS = 4
HEAD_DIM = 128
TOK_DEV = 256
TOKENS = 4096
MOST = 512
EPISODES = 16


def row_scales(scale_key, low, high):
    return jnp.exp(jax.random.uniform(scale_key, (TOKENS, 1), minval=math.log(low), maxval=math.log(high)))


def draw_keys(key, part):
    key = jax.random.fold_in(key, 5)
    scale_key, base_key = jax.random.split(key, 2)
    row_scale = row_scales(scale_key, 0.5, 1.5)
    base_draw = jax.random.normal(base_key, (TOKENS, KV_HEADS * HEAD_DIM))
    drawn_keys = jnp.clip(base_draw * row_scale, -6.0, 6.0)
    return drawn_keys.astype(jnp.bfloat16)


def draw_queries(key, part):
    key = jax.random.fold_in(key, 9)
    scale_key, base_key = jax.random.split(key)
    row_scale = row_scales(scale_key, 0.3, 3.0)
    base_draw = jax.random.normal(base_key, (TOKENS, HEADS * HEAD_DIM))
    drawn_queries = jnp.clip(base_draw * row_scale, -12.0, 12.0)
    return drawn_queries.astype(jnp.bfloat16)


def shard_levels(own_key, dims, cuts, smallest, largest):
    gain = 1.0
    for dim, parts in cuts:
        draws = jax.random.uniform(jax.random.fold_in(jax.random.fold_in(own_key, 6), dim), (parts,), jnp.float32, smallest / len(cuts), largest / len(cuts))
        gain = gain * jnp.repeat(jnp.exp(draws), dims[dim] // parts).reshape((-1,) + (1,) * (len(dims) - 1 - dim))
    return gain


def length_profile(count, total, bound, slope):
    portions = [(1 << 20) // math.isqrt(grade ** slope) + 1 for grade in range(2, count + 1)]
    surplus, given = total - bound - (count - 1), [1] * (count - 1)
    while surplus > 0:
        candidates = [i for i in range(count - 1) if given[i] < bound]
        pool, remaining = sum([portions[i] for i in candidates]), surplus
        for i in candidates:
            extra = min(bound - given[i], max(1, remaining * portions[i] // pool), surplus)
            given[i] = given[i] + extra
            surplus = surplus - extra
    return np.array([bound] + given)


def ragged_sizes(own_key, count, total, bound, slope):
    if count == 2:
        one = jax.random.randint(own_key, (), max(1, total - bound), min(bound, total - 1) + 1)
        return jnp.stack([one, total - one])
    lengths = jnp.asarray(length_profile(count, total, bound, slope), jnp.int32)
    twos = (count - 1) // 2
    donor, receiver = lengths[1:1 + 2 * twos:2], lengths[2:2 + 2 * twos:2]
    margin = jnp.minimum(donor - 1, bound - receiver)
    passed = jax.random.randint(jax.random.fold_in(own_key, 1), (twos,), 0, 1 << 20) % (margin + 1)
    lengths = lengths.at[1:1 + 2 * twos:2].set(donor - passed).at[2:2 + 2 * twos:2].set(receiver + passed)
    return lengths[jax.random.permutation(jax.random.fold_in(own_key, 2), count)]


def centred(stream_key, shape, width, bound, cuts=(), kind=jnp.bfloat16):
    level = shard_levels(stream_key, shape, cuts, -0.22, 0.18) if cuts else 1.0
    values = jax.random.normal(stream_key, shape, jnp.float32) * width * level
    return jnp.minimum(jnp.maximum(values, -bound), bound).astype(kind)


def setup_inputs(seed: int = 0, part: int = 0) -> dict:
    key_of = jax.random.split(jax.random.key(seed), 6)
    part_splits = jax.random.split(jax.random.fold_in(key_of[5], part), 6)
    queries = draw_queries(jax.random.fold_in(jax.random.fold_in(key_of[5], part), 71), part)
    keys = draw_keys(jax.random.fold_in(jax.random.fold_in(key_of[5], part), 71), part)
    values = centred(part_splits[2], (TOKENS, KV_HEADS * HEAD_DIM), 1.0, 6.0, ((0, 16),))
    grad_out = centred(part_splits[3], (TOKENS, HEADS * HEAD_DIM), 1.0, 6.0, ((0, 16),))
    episode_lengths = ragged_sizes(part_splits[4], EPISODES, TOKENS, MOST, 2).astype(jnp.int32)
    return dict(queries=queries, keys=keys, values=values, grad_out=grad_out, episode_lengths=episode_lengths)


def episode_of(episode_lengths, position):
    episode_ends = jnp.cumsum(episode_lengths).astype(jnp.int32)
    covered = lax.optimization_barrier(jnp.sum((episode_ends[None, :] <= position[:, None]).astype(jnp.int32), axis=1))
    return jnp.where(position < 0, -1, covered).astype(jnp.int32)

def reference(queries, keys, values, grad_out, episode_lengths):
    window = 2 * TOK_DEV
    blocks = TOKENS // window
    per_group = HEADS // KV_HEADS
    kv_width = KV_HEADS * HEAD_DIM
    factor = 1.0 / math.sqrt(HEAD_DIM)
    position = jnp.arange(TOKENS + window, dtype=jnp.int32) - window
    labels = episode_of(episode_lengths, position)
    zero_rows = jnp.zeros((window, kv_width), keys.dtype)
    keys_padded = jnp.concatenate([zero_rows, keys], axis=0)
    values_padded = jnp.concatenate([zero_rows, values], axis=0)
    query_local = window + jnp.arange(window, dtype=jnp.int32)
    key_local = jnp.arange(2 * window, dtype=jnp.int32)
    causal = key_local[None, :] <= query_local[:, None]

    def one_block(block_index):
        first_row = (block_index * window).astype(jnp.int32)
        query_block = lax.dynamic_slice_in_dim(queries, first_row, window, 0).astype(jnp.float32)
        query_block = query_block.reshape(window, KV_HEADS, per_group, HEAD_DIM)
        grad_block = lax.dynamic_slice_in_dim(grad_out, first_row, window, 0).astype(jnp.float32)
        grad_block = grad_block.reshape(window, KV_HEADS, per_group, HEAD_DIM)
        key_window = lax.dynamic_slice_in_dim(keys_padded, first_row, 2 * window, 0).astype(jnp.float32)
        key_window = key_window.reshape(2 * window, KV_HEADS, HEAD_DIM)
        value_window = lax.dynamic_slice_in_dim(values_padded, first_row, 2 * window, 0).astype(jnp.float32)
        value_window = value_window.reshape(2 * window, KV_HEADS, HEAD_DIM)
        query_label = lax.dynamic_slice_in_dim(labels, first_row + window, window, 0)
        key_label = lax.dynamic_slice_in_dim(labels, first_row, 2 * window, 0)
        allowed = (query_label[:, None] == key_label[None, :]) & causal
        scores = jnp.einsum('igrd,jgd->grij', query_block, key_window) * factor
        masked = jnp.where(allowed[None, None], scores, -jnp.inf)
        row_max = lax.optimization_barrier(jnp.max(masked, axis=3, keepdims=True))
        log_total = row_max + jnp.log(lax.optimization_barrier(jnp.sum(jnp.exp(masked - row_max), axis=3, keepdims=True)))
        soft_probs = jnp.exp(masked - log_total)
        weights = lax.optimization_barrier(soft_probs.astype(jnp.bfloat16))
        weights_wide = weights.astype(jnp.float32)
        attended = jnp.einsum('grij,jgd->igrd', weights_wide, value_window).astype(jnp.bfloat16)
        grad_probs = jnp.einsum('igrd,jgd->grij', grad_block, value_window)
        row_delta = jnp.einsum('igrd,igrd->gri', grad_block, attended.astype(jnp.float32))
        grad_scores = lax.optimization_barrier((soft_probs * (grad_probs - row_delta[..., None])).astype(jnp.bfloat16))
        grad_wide = grad_scores.astype(jnp.float32)
        grad_query = (jnp.einsum('grij,jgd->igrd', grad_wide, key_window) * factor).astype(jnp.bfloat16)
        grad_key = jnp.einsum('grij,igrd->jgd', grad_wide, query_block)
        grad_value = jnp.einsum('grij,igrd->jgd', weights_wide, grad_block)
        return (attended.reshape(window, HEADS * HEAD_DIM), grad_query.reshape(window, HEADS * HEAD_DIM), grad_key.reshape(2 * window, kv_width), grad_value.reshape(2 * window, kv_width))
    results = lax.map(one_block, jnp.arange(blocks, dtype=jnp.int32))
    attn_out = results[0].reshape(TOKENS, HEADS * HEAD_DIM)
    grad_queries = results[1].reshape(TOKENS, HEADS * HEAD_DIM)

    def combine(terms):
        halves = terms.reshape(blocks, 2, window, kv_width)
        following = jnp.concatenate([halves[1:, 0], jnp.zeros((1, window, kv_width), jnp.float32)], axis=0)
        return (halves[:, 1] + following).reshape(TOKENS, kv_width)
    grad_keys = (combine(results[2]) * factor).astype(jnp.bfloat16)
    grad_values = combine(results[3]).astype(jnp.bfloat16)
    return (attn_out, grad_queries, grad_keys, grad_values)
```

```python
import functools
import math

import jax
import jax.numpy as jnp
from jax import lax
from jax.experimental import pallas as pl
from jax.experimental.pallas import tpu as pltpu
from jax.sharding import PartitionSpec as P

HEAD_DIM = 128
TILE = 128
HEADS_AT_ONCE = 4
CHUNKS = 2
NT = (((1,), (1,)), ((), ()))
NN = (((1,), (0,)), ((), ()))
TN = (((0,), (0,)), ((), ()))
FACTOR = 1.0 / math.sqrt(HEAD_DIM)
FACTOR2 = math.log2(math.e) / math.sqrt(HEAD_DIM)
NEVER = -1e30


def matmul(left, right, dims):
    return lax.dot_general(left, right, dims, preferred_element_type=jnp.float32)


def permuted(value, pairs):
    return lax.ppermute(value, "seq", pairs)


def attention_kernel(count, aliased, lengths_ref, first_ref, *refs):
    refs = refs[2:] if aliased else refs
    (q_ref, do_ref, far_k, near_k, own_k, far_v, near_v, own_v) = refs[:8]
    o_ref, dq_ref, back_ref, dk_ref, dv_ref, k_all, v_all, bias, dk_sum, dv_sum = refs[8:]
    rows = q_ref.shape[0]
    heads = q_ref.shape[1] // HEAD_DIM
    tiles = rows // TILE
    band = 2 * rows + TILE
    per_call = min(HEADS_AT_ONCE, heads)
    for place, (k_ref, v_ref) in enumerate(((far_k, far_v), (near_k, near_v), (own_k, own_v))):
        k_all[place * rows : (place + 1) * rows] = k_ref[...]
        v_all[place * rows : (place + 1) * rows] = v_ref[...]

    @pl.when(pl.program_id(0) == 0)
    def _():
        row = lax.broadcasted_iota(jnp.int32, (rows, 1), 0)

        def one(index, carry):
            begin, start = carry
            return begin + lengths_ref[index], jnp.where(row >= begin, begin, start)

        _, start = lax.fori_loop(
            0, count, one, (-first_ref[0], jnp.full((rows, 1), -4 * rows, jnp.int32))
        )
        for tile in range(tiles):
            here = slice(tile * TILE, (tile + 1) * TILE)
            key = lax.broadcasted_iota(jnp.int32, (TILE, band), 1) + (tile * TILE - 2 * rows)
            allowed = (key >= start[here]) & (key <= row[here])
            bias[tile] = jnp.where(allowed, 0.0, NEVER)

    dk_sum[...] = jnp.zeros_like(dk_sum)
    dv_sum[...] = jnp.zeros_like(dv_sum)
    for tile in range(tiles):
        here = slice(tile * TILE, (tile + 1) * TILE)
        keys = slice(tile * TILE, tile * TILE + band)
        k = k_all[keys]
        v = v_all[keys]
        for first in range(0, heads, per_call):
            cols = [slice((first + x) * HEAD_DIM, (first + x + 1) * HEAD_DIM) for x in range(per_call)]
            q = jnp.concatenate([q_ref[here, c] for c in cols], 0)
            do = jnp.concatenate([do_ref[here, c] for c in cols], 0)
            s = matmul(q, k, NT).reshape(per_call, TILE, band)
            s = (s * FACTOR2 + bias[tile][None]).reshape(per_call * TILE, band)
            e = jnp.exp2(s - jnp.max(s, 1, keepdims=True))
            prob = e * (1.0 / jnp.sum(e, 1, keepdims=True))
            weight = prob.astype(jnp.bfloat16)
            out = matmul(weight, v, NN).astype(jnp.bfloat16)
            dp = matmul(do, v, NT)
            delta = jnp.sum(out.astype(jnp.float32) * do.astype(jnp.float32), 1, keepdims=True)
            ds = (prob * (dp - delta)).astype(jnp.bfloat16)
            dq = (matmul(ds, k, NN) * FACTOR).astype(jnp.bfloat16)
            for x, c in enumerate(cols):
                o_ref[here, c] = out[x * TILE : (x + 1) * TILE]
                dq_ref[here, c] = dq[x * TILE : (x + 1) * TILE]
            dv_sum[keys] += matmul(weight, do, TN)
            dk_sum[keys] += matmul(ds, q, TN)
    dk_ref[...] = dk_sum[2 * rows :] * FACTOR
    dv_ref[...] = dv_sum[2 * rows :]
    for place in range(2):
        span = slice(place * rows, (place + 1) * rows)
        back_ref[place, 0] = (dk_sum[span] * FACTOR).astype(jnp.bfloat16)
        back_ref[place, 1] = dv_sum[span].astype(jnp.bfloat16)


def attention(chunk, groups, lengths, first, q, do, far, near, own_k, own_v, carried):
    rows, width = q.shape
    head_cols = width // (own_k.shape[1] // HEAD_DIM)
    base = chunk * groups
    kv = pl.BlockSpec((rows, HEAD_DIM), lambda g: (0, base + g))
    wide = pl.BlockSpec((rows, head_cols), lambda g: (0, base + g))
    sent_k = pl.BlockSpec((rows, HEAD_DIM), lambda g: (0, g))
    sent_v = pl.BlockSpec((rows, HEAD_DIM), lambda g: (0, groups + g))
    part = pl.BlockSpec((rows, HEAD_DIM), lambda g: (0, g))
    smem = pl.BlockSpec(memory_space=pltpu.SMEM)
    kept = pl.BlockSpec(memory_space=pl.ANY)
    aliased = carried is not None
    carried = carried if aliased else ()
    return pl.pallas_call(
        functools.partial(attention_kernel, lengths.shape[0], aliased),
        grid=(groups,),
        in_specs=[smem, smem] + [kept] * len(carried) + [wide, wide, sent_k, sent_k, kv, sent_v, sent_v, kv],
        out_specs=[
            wide,
            wide,
            pl.BlockSpec((2, 2, rows, HEAD_DIM), lambda g: (0, 0, 0, g)),
            part,
            part,
        ],
        out_shape=[
            jax.ShapeDtypeStruct(q.shape, jnp.bfloat16),
            jax.ShapeDtypeStruct(q.shape, jnp.bfloat16),
            jax.ShapeDtypeStruct((2, 2, rows, groups * HEAD_DIM), jnp.bfloat16),
            jax.ShapeDtypeStruct((rows, groups * HEAD_DIM), jnp.float32),
            jax.ShapeDtypeStruct((rows, groups * HEAD_DIM), jnp.float32),
        ],
        scratch_shapes=[
            pltpu.VMEM((3 * rows, HEAD_DIM), jnp.bfloat16),
            pltpu.VMEM((3 * rows, HEAD_DIM), jnp.bfloat16),
            pltpu.VMEM((rows // TILE, TILE, 2 * rows + TILE), jnp.float32),
            pltpu.VMEM((3 * rows, HEAD_DIM), jnp.float32),
            pltpu.VMEM((3 * rows, HEAD_DIM), jnp.float32),
        ],
        input_output_aliases={2: 0, 3: 1} if aliased else {},
        compiler_params=pltpu.CompilerParams(vmem_limit_bytes=48 * 1024 * 1024),
        cost_estimate=pl.CostEstimate(
            flops=12 * rows * 3 * rows * head_cols * groups,
            bytes_accessed=8 * rows * head_cols * groups,
            transcendentals=0,
        ),
        name="attention",
    )(lengths, first, *carried, q, do, far, near, own_k, far, near, own_v)


def on_device(queries, keys, values, grad_out, episode_lengths):
    rows = queries.shape[0]
    groups = keys.shape[1] // HEAD_DIM
    count = lax.axis_size("seq")
    place = lax.axis_index("seq")
    odd = place % 2 == 1
    first = jnp.reshape(place * rows, (1,)).astype(jnp.int32)
    ahead = [(source, source + 2) for source in range(count - 2)]
    behind = [(source + 2, source) for source in range(count - 2)]
    swap = [(source, source ^ 1) for source in range(count)]
    chunks = CHUNKS if groups % CHUNKS == 0 else 1
    per_chunk = groups // chunks
    cols = per_chunk * HEAD_DIM

    own = []
    for chunk in range(chunks):
        span = slice(chunk * cols, (chunk + 1) * cols)
        own.append(jnp.concatenate([keys[:, span], values[:, span]], axis=1))
    far = [permuted(block, ahead) for block in own]
    carried = None
    grads = []
    for chunk in range(chunks):
        near = permuted(jnp.where(odd, far[chunk], own[chunk]), swap)
        attn_out, grad_queries, back, dk, dv = attention(
            chunk, per_chunk, episode_lengths, first, queries, grad_out, far[chunk], near, keys, values, carried
        )
        carried = (attn_out, grad_queries)
        beside = permuted(back[1], swap)
        zero = jnp.zeros_like(beside)
        onward = back[0].astype(jnp.float32) + jnp.where(odd, beside, zero).astype(jnp.float32)
        returned = permuted(onward.astype(jnp.bfloat16), behind)
        extra = returned.astype(jnp.float32) + jnp.where(odd, zero, beside).astype(jnp.float32)
        grads.append(((dk + extra[0]).astype(jnp.bfloat16), (dv + extra[1]).astype(jnp.bfloat16)))
    grad_keys = jnp.concatenate([pair[0] for pair in grads], axis=1)
    grad_values = jnp.concatenate([pair[1] for pair in grads], axis=1)
    return (attn_out, grad_queries, grad_keys, grad_values)


def solution(mesh):
    split = P(("groups", "seq"), None)
    return jax.shard_map(
        on_device,
        mesh=mesh,
        in_specs=(split, split, split, split, P("groups")),
        out_specs=(split, split, split, split),
        check_vma=False,
    )
```

```python
import functools
import math

import jax
import jax.numpy as jnp
from jax import lax
from jax.experimental import pallas as pl
from jax.experimental.pallas import tpu as pltpu
from jax.sharding import PartitionSpec as P

HEAD_DIM = 128
TILE = 128
HEADS_AT_ONCE = 4
SPLIT = (2, 2)
NT = (((1,), (1,)), ((), ()))
NN = (((1,), (0,)), ((), ()))
TN = (((0,), (0,)), ((), ()))
FACTOR = 1.0 / math.sqrt(HEAD_DIM)
FACTOR2 = math.log2(math.e) / math.sqrt(HEAD_DIM)
NEVER = -1e30
VMEM_LIMIT = 40 * 1024 * 1024
SMALL_LIMIT = 6 * 1024 * 1024


def matmul(left, right, dims):
    return lax.dot_general(left, right, dims, preferred_element_type=jnp.float32)


def permuted(value, pairs):
    return lax.ppermute(value, "seq", pairs)


def in_hbm(value):
    return pltpu.with_memory_space_constraint(value, pltpu.HBM)


def pack_kernel(starts, sizes, k_ref, v_ref, *outs):
    for out, start, size in zip(outs, starts, sizes):
        out[:, :size] = k_ref[:, start : start + size]
        out[:, size:] = v_ref[:, start : start + size]


def packed(keys, values, starts, sizes):
    rows = keys.shape[0]
    return pl.pallas_call(
        functools.partial(pack_kernel, starts, sizes),
        grid=(1,),
        in_specs=[pl.BlockSpec(keys.shape, lambda i: (0, 0))] * 2,
        out_specs=[pl.BlockSpec((rows, 2 * size), lambda i: (0, 0)) for size in sizes],
        out_shape=[jax.ShapeDtypeStruct((rows, 2 * size), keys.dtype) for size in sizes],
        compiler_params=pltpu.CompilerParams(vmem_limit_bytes=SMALL_LIMIT),
        name="pack_keys_values",
    )(keys, values)


def mask_kernel(count, lengths_ref, first_ref, bias_ref):
    tiles, _, band = bias_ref.shape
    rows = tiles * TILE
    row = lax.broadcasted_iota(jnp.int32, (rows, 1), 0)

    def one(index, carry):
        begin, start = carry
        return begin + lengths_ref[index], jnp.where(row >= begin, begin, start)

    _, start = lax.fori_loop(
        0, count, one, (-first_ref[0], jnp.full((rows, 1), -4 * rows, jnp.int32))
    )
    for tile in range(tiles):
        here = slice(tile * TILE, (tile + 1) * TILE)
        key = lax.broadcasted_iota(jnp.int32, (TILE, band), 1) + (tile * TILE - 2 * rows)
        allowed = (key >= start[here]) & (key <= row[here])
        bias_ref[tile] = jnp.where(allowed, 0.0, NEVER)


def masks(rows, lengths, first):
    smem = pl.BlockSpec(memory_space=pltpu.SMEM)
    return pl.pallas_call(
        functools.partial(mask_kernel, lengths.shape[0]),
        in_specs=[smem, smem],
        out_specs=pl.BlockSpec(memory_space=pltpu.VMEM),
        out_shape=jax.ShapeDtypeStruct((rows // TILE, TILE, 2 * rows + TILE), jnp.float32),
        compiler_params=pltpu.CompilerParams(vmem_limit_bytes=SMALL_LIMIT),
        name="masks",
    )(lengths, first)


def gather_rows(all_ref, parts):
    rows = parts[0].shape[0]
    for place, part in enumerate(parts):
        all_ref[place * rows : (place + 1) * rows] = part[...]


def unit_slices(unit, per_call, band):
    tile, first = unit
    here = slice(tile * TILE, (tile + 1) * TILE)
    keys = slice(tile * TILE, tile * TILE + band)
    cols = [slice((first + x) * HEAD_DIM, (first + x + 1) * HEAD_DIM) for x in range(per_call)]
    return here, keys, cols


def stacked(ref, here, cols):
    return jnp.concatenate([ref[here, c] for c in cols], 0)


def attention_kernel(aliased, *refs):
    refs = refs[2:] if aliased else refs
    (bias, q_ref, do_ref, far_k, near_k, own_k, far_v, near_v, own_v) = refs[:9]
    o_ref, dq_ref, back_ref, own_ref, k_all, v_all, dk_sum, dv_sum = refs[9:]
    rows = q_ref.shape[0]
    heads = q_ref.shape[1] // HEAD_DIM
    band = 2 * rows + TILE
    per_call = min(HEADS_AT_ONCE, heads)
    gather_rows(k_all, (far_k, near_k, own_k))
    gather_rows(v_all, (far_v, near_v, own_v))
    dk_sum[...] = jnp.zeros_like(dk_sum)
    dv_sum[...] = jnp.zeros_like(dv_sum)
    units = [(tile, first) for tile in range(rows // TILE) for first in range(0, heads, per_call)]

    def scores(unit):
        here, keys, cols = unit_slices(unit, per_call, band)
        return matmul(stacked(q_ref, here, cols), k_all[keys], NT)

    def softmax(unit, s):
        s = s.reshape(per_call, TILE, band) * FACTOR2 + bias[unit[0]][None]
        s = s.reshape(per_call * TILE, band)
        e = jnp.exp2(s - jnp.max(s, 1, keepdims=True))
        return e * (1.0 / jnp.sum(e, 1, keepdims=True))

    def score_grads(unit, prob, weight):
        here, keys, cols = unit_slices(unit, per_call, band)
        do = stacked(do_ref, here, cols)
        out = matmul(weight, v_all[keys], NN).astype(jnp.bfloat16)
        for x, c in enumerate(cols):
            o_ref[here, c] = out[x * TILE : (x + 1) * TILE]
        dp = matmul(do, v_all[keys], NT)
        delta = jnp.sum(out.astype(jnp.float32) * do.astype(jnp.float32), 1, keepdims=True)
        return (prob * (dp - delta)).astype(jnp.bfloat16)

    def sums(unit, weight, ds):
        here, keys, cols = unit_slices(unit, per_call, band)
        dq = (matmul(ds, k_all[keys], NN) * FACTOR).astype(jnp.bfloat16)
        for x, c in enumerate(cols):
            dq_ref[here, c] = dq[x * TILE : (x + 1) * TILE]
        dv_sum[:, keys] += matmul(stacked(do_ref, here, cols), weight, TN)
        dk_sum[:, keys] += matmul(stacked(q_ref, here, cols), ds, TN)

    ahead = scores(units[0])
    before = None
    for index, unit in enumerate(units):
        now = ahead
        if index + 1 < len(units):
            ahead = scores(units[index + 1])
        prob = softmax(unit, now)
        weight = prob.astype(jnp.bfloat16)
        if before is not None:
            sums(*before)
        before = (unit, weight, score_grads(unit, prob, weight))
    sums(*before)

    own_ref[0] = dk_sum[:, 2 * rows :].T * FACTOR
    own_ref[1] = dv_sum[:, 2 * rows :].T
    for place in range(2):
        span = slice(place * rows, (place + 1) * rows)
        back_ref[place, 0] = (dk_sum[:, span].T * FACTOR).astype(jnp.bfloat16)
        back_ref[place, 1] = dv_sum[:, span].T.astype(jnp.bfloat16)


def attention(base, groups, bias, q, do, far, near, own_k, own_v, carried):
    rows, width = q.shape
    head_cols = width // (own_k.shape[1] // HEAD_DIM)
    own = pl.BlockSpec((rows, HEAD_DIM), lambda g: (0, base + g))
    sent_k = pl.BlockSpec((rows, HEAD_DIM), lambda g: (0, g))
    sent_v = pl.BlockSpec((rows, HEAD_DIM), lambda g: (0, groups + g))
    wide = pl.BlockSpec((rows, head_cols), lambda g: (0, base + g))
    aliased = carried is not None
    carried = carried if aliased else ()
    return pl.pallas_call(
        functools.partial(attention_kernel, aliased),
        grid=(groups,),
        in_specs=[pl.BlockSpec(memory_space=pl.ANY)] * len(carried)
        + [pl.BlockSpec(bias.shape, lambda g: (0, 0, 0)), wide, wide]
        + [sent_k, sent_k, own, sent_v, sent_v, own],
        out_specs=[
            wide,
            wide,
            pl.BlockSpec((2, 2, rows, HEAD_DIM), lambda g: (0, 0, 0, g)),
            pl.BlockSpec((2, rows, HEAD_DIM), lambda g: (0, 0, g)),
        ],
        out_shape=[
            jax.ShapeDtypeStruct(q.shape, jnp.bfloat16),
            jax.ShapeDtypeStruct(q.shape, jnp.bfloat16),
            jax.ShapeDtypeStruct((2, 2, rows, groups * HEAD_DIM), jnp.bfloat16),
            jax.ShapeDtypeStruct((2, rows, groups * HEAD_DIM), jnp.float32),
        ],
        scratch_shapes=[
            pltpu.VMEM((3 * rows, HEAD_DIM), jnp.bfloat16),
            pltpu.VMEM((3 * rows, HEAD_DIM), jnp.bfloat16),
            pltpu.VMEM((HEAD_DIM, 3 * rows), jnp.float32),
            pltpu.VMEM((HEAD_DIM, 3 * rows), jnp.float32),
        ],
        input_output_aliases={0: 0, 1: 1} if aliased else {},
        compiler_params=pltpu.CompilerParams(vmem_limit_bytes=VMEM_LIMIT),
        name="attention",
    )(*carried, bias, q, do, far, near, own_k, far, near, own_v)


def finish_kernel(aliased, *refs):
    refs = refs[2:] if aliased else refs
    kept_ref, returned_ref, gk_ref, gv_ref = refs
    gk_ref[...] = (kept_ref[0] + returned_ref[0].astype(jnp.float32)).astype(jnp.bfloat16)
    gv_ref[...] = (kept_ref[1] + returned_ref[1].astype(jnp.float32)).astype(jnp.bfloat16)


def finished(chunk, shape, kept, returned, carried):
    aliased = carried is not None
    carried = carried if aliased else ()
    out = pl.BlockSpec((shape[0], kept.shape[2]), lambda i: (0, chunk))
    return pl.pallas_call(
        functools.partial(finish_kernel, aliased),
        grid=(1,),
        in_specs=[pl.BlockSpec(memory_space=pl.ANY)] * len(carried)
        + [pl.BlockSpec(kept.shape, lambda i: (0, 0, 0))] * 2,
        out_specs=[out, out],
        out_shape=[jax.ShapeDtypeStruct(shape, jnp.bfloat16)] * 2,
        input_output_aliases={0: 0, 1: 1} if aliased else {},
        compiler_params=pltpu.CompilerParams(vmem_limit_bytes=SMALL_LIMIT),
        name="finish_keys_values",
    )(*carried, kept, returned)


def on_device(queries, keys, values, grad_out, episode_lengths):
    rows = queries.shape[0]
    groups = keys.shape[1] // HEAD_DIM
    count = lax.axis_size("seq")
    place = lax.axis_index("seq").astype(jnp.int32)
    odd = lax.bitwise_and(place, jnp.int32(1))
    first = jnp.reshape(place * rows, (1,))
    ahead = [(source, (source + 2) % count) for source in range(count)]
    behind = [((source + 2) % count, source) for source in range(count)]
    swap = [(source, source ^ 1) for source in range(count)]
    split = SPLIT if sum(SPLIT) == groups else (groups,)
    bases = [sum(split[:index]) for index in range(len(split))]

    own = list(packed(keys, values, [b * HEAD_DIM for b in bases], [s * HEAD_DIM for s in split]))
    far = [permuted(block, ahead) for block in own]
    bias = masks(rows, episode_lengths, first)
    own[0], bias = lax.optimization_barrier((own[0], bias))
    q_here, do_here, k_here, v_here = (in_hbm(x) for x in (queries, grad_out, keys, values))
    carried = grads = None
    parts = []
    for index, (base, size) in enumerate(zip(bases, split)):
        near = permuted(jnp.where(odd == 1, far[index], own[index]), swap)
        attn_out, grad_queries, back, kept = attention(
            base, size, bias, q_here, do_here, far[index], near, k_here, v_here, carried
        )
        carried = (attn_out, grad_queries)
        if parts:
            back, parts[-1][1] = lax.optimization_barrier((back, parts[-1][1]))
        beside = permuted(back[1], swap)
        none = jnp.zeros_like(beside)
        onward = back[0].astype(jnp.float32) + jnp.where(odd == 1, beside, none).astype(jnp.float32)
        kept = kept + jnp.where(odd == 1, none, beside).astype(jnp.float32)
        parts.append([kept, permuted(onward.astype(jnp.bfloat16), behind)])
    for base, size, (kept, returned) in zip(bases, split, parts):
        grads = finished(base // size, keys.shape, kept, returned, grads)
    return (attn_out, grad_queries, *grads)


def solution(mesh):
    split = P(("groups", "seq"), None)
    return jax.shard_map(
        on_device,
        mesh=mesh,
        in_specs=(split, split, split, split, P("groups")),
        out_specs=(split, split, split, split),
        check_vma=False,
    )
```

```python
import functools
import math

import jax
import jax.numpy as jnp
from jax import lax
from jax.experimental import pallas as pl
from jax.experimental.pallas import tpu as pltpu
from jax.sharding import PartitionSpec as P

HEAD_DIM = 128
TILE = 128
HEADS_AT_ONCE = 4
SENT = (2, 2)
CALLS = (2, 2)
RETURNED = (2, 2)
NT = (((1,), (1,)), ((), ()))
NN = (((1,), (0,)), ((), ()))
TN = (((0,), (0,)), ((), ()))
FACTOR = 1.0 / math.sqrt(HEAD_DIM)
FACTOR2 = math.log2(math.e) / math.sqrt(HEAD_DIM)
NEVER = -1e30
VMEM_LIMIT = 20 * 1024 * 1024
QUERY_LIMIT = 12 * 1024 * 1024
SMALL_LIMIT = 6 * 1024 * 1024


def matmul(left, right, dims):
    return lax.dot_general(left, right, dims, preferred_element_type=jnp.float32)


def permuted(value, pairs):
    return lax.ppermute(value, "seq", pairs)


def in_hbm(value):
    return pltpu.with_memory_space_constraint(value, pltpu.HBM)


def pack_kernel(starts, sizes, k_ref, v_ref, *outs):
    for out, start, size in zip(outs, starts, sizes):
        out[:, :size] = k_ref[:, start : start + size]
        out[:, size:] = v_ref[:, start : start + size]


def packed(keys, values, starts, sizes):
    rows = keys.shape[0]
    return pl.pallas_call(
        functools.partial(pack_kernel, starts, sizes),
        grid=(1,),
        in_specs=[pl.BlockSpec(keys.shape, lambda i: (0, 0))] * 2,
        out_specs=[pl.BlockSpec((rows, 2 * size), lambda i: (0, 0)) for size in sizes],
        out_shape=[jax.ShapeDtypeStruct((rows, 2 * size), keys.dtype) for size in sizes],
        compiler_params=pltpu.CompilerParams(vmem_limit_bytes=SMALL_LIMIT),
        name="pack_keys_values",
    )(keys, values)


def mask_kernel(count, lengths_ref, first_ref, bias_ref):
    tiles, _, band = bias_ref.shape
    rows = tiles * TILE
    row = lax.broadcasted_iota(jnp.int32, (rows, 1), 0)

    def one(index, carry):
        begin, start = carry
        return begin + lengths_ref[index], jnp.where(row >= begin, begin, start)

    _, start = lax.fori_loop(
        0, count, one, (-first_ref[0], jnp.full((rows, 1), -4 * rows, jnp.int32))
    )
    for tile in range(tiles):
        here = slice(tile * TILE, (tile + 1) * TILE)
        key = lax.broadcasted_iota(jnp.int32, (TILE, band), 1) + (tile * TILE - 2 * rows)
        allowed = (key >= start[here]) & (key <= row[here])
        bias_ref[tile] = jnp.where(allowed, 0.0, NEVER)


def masks(rows, lengths, first):
    smem = pl.BlockSpec(memory_space=pltpu.SMEM)
    return pl.pallas_call(
        functools.partial(mask_kernel, lengths.shape[0]),
        in_specs=[smem, smem],
        out_specs=pl.BlockSpec(memory_space=pltpu.VMEM),
        out_shape=jax.ShapeDtypeStruct((rows // TILE, TILE, 2 * rows + TILE), jnp.float32),
        compiler_params=pltpu.CompilerParams(vmem_limit_bytes=SMALL_LIMIT),
        name="masks",
    )(lengths, first)


def lanes(block, width=HEAD_DIM):
    return pl.ds(pl.multiple_of(block * width, width), width)


def attention_kernel(base, skipped, first_ref, bias, q_hbm, do_hbm, far, near, own, *refs):
    o_ref, ds_ref, back_ref, own_ref, q_ref, do_ref, k_all, v_all, dk_sum, dv_sum, sems = refs
    group = pl.program_id(0)
    groups, tiles, _, _ = ds_ref.shape
    rows = far.shape[0]
    sent = far.shape[1] // (2 * HEAD_DIM)
    wide = q_ref.shape[2]
    heads = wide // HEAD_DIM
    per_call = min(HEADS_AT_ONCE, heads)

    def fetches(index):
        span = pl.ds((base + index) * wide, wide)
        return [
            pltpu.make_async_copy(whole.at[:, span], held.at[index], sems.at[index, place])
            for place, (whole, held) in enumerate(((q_hbm, q_ref), (do_hbm, do_ref)))
        ]

    @pl.when(group == 0)
    def _():
        for index in range(groups):
            for fetch in fetches(index):
                fetch.start()

    k_col = lanes(skipped + group)
    v_col = lanes(sent + skipped + group)
    for place, part in enumerate((far, near, own)):
        k_all[place * rows : (place + 1) * rows] = part[:, k_col]
        v_all[place * rows : (place + 1) * rows] = part[:, v_col]
    for index in range(groups):

        @pl.when(group == index)
        def _():
            for fetch in fetches(index):
                fetch.wait()

    def all_units(lowest):
        dk_sum[...] = jnp.zeros_like(dk_sum)
        dv_sum[...] = jnp.zeros_like(dv_sum)
        units = [(tile, first) for tile in range(tiles) for first in range(0, heads, per_call)]

        def places(unit):
            tile, first = unit
            here = slice(tile * TILE, (tile + 1) * TILE)
            keys = slice(max(tile * TILE, lowest), tile * TILE + 2 * rows + TILE)
            cols = [slice((first + x) * HEAD_DIM, (first + x + 1) * HEAD_DIM) for x in range(per_call)]
            return here, keys, cols

        def stacked(ref, unit):
            here, _, cols = places(unit)
            return jnp.concatenate([ref[group, here, c] for c in cols], 0)

        def scores(unit):
            return matmul(stacked(q_ref, unit), k_all[places(unit)[1]], NT)

        def softmax(unit, s):
            _, keys, _ = places(unit)
            width = keys.stop - keys.start
            shut = bias[unit[0], :, keys.start - unit[0] * TILE :]
            s = s.reshape(per_call, TILE, width) * FACTOR2 + shut[None]
            s = s.reshape(per_call * TILE, width)
            e = jnp.exp2(s - jnp.max(s, 1, keepdims=True))
            return e * (1.0 / jnp.sum(e, 1, keepdims=True))

        def score_grads(unit, prob, weight):
            here, keys, cols = places(unit)
            do = stacked(do_ref, unit)
            out = matmul(weight, v_all[keys], NN).astype(jnp.bfloat16)
            for x, c in enumerate(cols):
                o_ref[group, here, c] = out[x * TILE : (x + 1) * TILE]
            dp = matmul(do, v_all[keys], NT)
            delta = jnp.sum(out.astype(jnp.float32) * do.astype(jnp.float32), 1, keepdims=True)
            ds = (prob * (dp - delta)).astype(jnp.bfloat16)
            tile, first = unit
            ds_ref[group, tile, first * TILE : (first + per_call) * TILE, keys.start - tile * TILE :] = ds
            return ds

        def sums(unit, weight, ds):
            _, keys, _ = places(unit)
            dv_sum[:, keys] += matmul(stacked(do_ref, unit), weight, TN)
            dk_sum[:, keys] += matmul(stacked(q_ref, unit), ds, TN)

        ahead = scores(units[0])
        before = None
        for index, unit in enumerate(units):
            now = ahead
            if index + 1 < len(units):
                ahead = scores(units[index + 1])
            prob = softmax(unit, now)
            weight = prob.astype(jnp.bfloat16)
            if before is not None:
                sums(*before)
            before = (unit, weight, score_grads(unit, prob, weight))
        sums(*before)
        if lowest:
            for tile in range(tiles):
                gap = max(0, lowest - tile * TILE)
                ds_ref[group, tile, :, :gap] = jnp.zeros((heads * TILE, gap), jnp.bfloat16)

        here = lanes(group)
        own_ref[0, :, here] = dk_sum[:, 2 * rows :].T * FACTOR
        own_ref[1, :, here] = dv_sum[:, 2 * rows :].T
        for place in range(2):
            span = slice(place * rows, (place + 1) * rows)
            back_ref[place, 0, :, here] = (dk_sum[:, span].T * FACTOR).astype(jnp.bfloat16)
            back_ref[place, 1, :, here] = dv_sum[:, span].T.astype(jnp.bfloat16)

    @pl.when(first_ref[0] >= 2 * rows)
    def _():
        all_units(0)

    @pl.when(first_ref[0] < 2 * rows)
    def _():
        all_units(rows)


def attention(base, groups, skipped, head_cols, first, bias, q, do, far, near, own):
    rows = q.shape[0]
    tiles, _, band = bias.shape
    whole = pl.BlockSpec(memory_space=pltpu.VMEM)
    far_away = pl.BlockSpec(memory_space=pltpu.HBM)
    return pl.pallas_call(
        functools.partial(attention_kernel, base, skipped),
        grid=(groups,),
        in_specs=[pl.BlockSpec(memory_space=pltpu.SMEM), whole, far_away, far_away, whole, whole, whole],
        out_specs=[whole] * 4,
        out_shape=[
            jax.ShapeDtypeStruct((groups, rows, head_cols), jnp.bfloat16),
            jax.ShapeDtypeStruct((groups, tiles, head_cols // HEAD_DIM * TILE, band), jnp.bfloat16),
            jax.ShapeDtypeStruct((2, 2, rows, groups * HEAD_DIM), jnp.bfloat16),
            jax.ShapeDtypeStruct((2, rows, groups * HEAD_DIM), jnp.float32),
        ],
        scratch_shapes=[
            pltpu.VMEM((groups, rows, head_cols), jnp.bfloat16),
            pltpu.VMEM((groups, rows, head_cols), jnp.bfloat16),
            pltpu.VMEM((3 * rows, HEAD_DIM), jnp.bfloat16),
            pltpu.VMEM((3 * rows, HEAD_DIM), jnp.bfloat16),
            pltpu.VMEM((HEAD_DIM, 3 * rows), jnp.float32),
            pltpu.VMEM((HEAD_DIM, 3 * rows), jnp.float32),
            pltpu.SemaphoreType.DMA((groups, 2)),
        ],
        compiler_params=pltpu.CompilerParams(vmem_limit_bytes=VMEM_LIMIT),
        name="attention",
    )(first, bias, q, do, far, near, own)


def query_kernel(calls, skips, *refs):
    o_out, dq_out, k_all = refs[-3:]
    group = pl.program_id(0)
    rows = o_out.shape[0]
    heads = o_out.shape[1] // HEAD_DIM
    base = 0
    for index, (size, skipped) in enumerate(zip(calls, skips)):
        o_ref, ds_ref, far, near, own = refs[5 * index : 5 * index + 5]

        @pl.when((group >= base) & (group < base + size))
        def _(base=base, skipped=skipped, o_ref=o_ref, ds_ref=ds_ref, parts=(far, near, own)):
            here = group - base
            o_out[...] = o_ref[here]
            for place, part in enumerate(parts):
                k_all[place * rows : (place + 1) * rows] = part[:, lanes(skipped + here)]
            for tile in range(ds_ref.shape[1]):
                k = k_all[tile * TILE : tile * TILE + ds_ref.shape[3]]
                dq = (matmul(ds_ref[here, tile], k, NN) * FACTOR).astype(jnp.bfloat16)
                for x in range(heads):
                    dq_out[tile * TILE : (tile + 1) * TILE, x * HEAD_DIM : (x + 1) * HEAD_DIM] = dq[
                        x * TILE : (x + 1) * TILE
                    ]

        base += size


def query_grads(calls, skips, shape, parts):
    rows, width = shape
    flat = [array for part in parts for array in part]
    out = pl.BlockSpec((rows, width // sum(calls)), lambda g: (0, g))
    return pl.pallas_call(
        functools.partial(query_kernel, calls, skips),
        grid=(sum(calls),),
        in_specs=[pl.BlockSpec(memory_space=pltpu.VMEM)] * len(flat),
        out_specs=[out, out],
        out_shape=[jax.ShapeDtypeStruct(shape, jnp.bfloat16)] * 2,
        scratch_shapes=[pltpu.VMEM((3 * rows, HEAD_DIM), jnp.bfloat16)],
        compiler_params=pltpu.CompilerParams(vmem_limit_bytes=QUERY_LIMIT),
        name="query_grads",
    )(*flat)


def finish_kernel(base, aliased, *refs):
    refs = refs[2:] if aliased else refs
    kept_ref, returned_ref, gk_ref, gv_ref, total, sems = refs
    span = pl.ds(base * HEAD_DIM, kept_ref.shape[2])
    copies = []
    for index, out in enumerate((gk_ref, gv_ref)):
        total[index] = (kept_ref[index] + returned_ref[index].astype(jnp.float32)).astype(jnp.bfloat16)
        copies.append(pltpu.make_async_copy(total.at[index], out.at[:, span], sems.at[index]))
        copies[-1].start()
    for copy in copies:
        copy.wait()


def finished(base, shape, kept, returned, carried):
    aliased = carried is not None
    carried = carried if aliased else ()
    kept_place = pl.BlockSpec(memory_space=pl.ANY)
    whole = pl.BlockSpec(memory_space=pltpu.VMEM)
    return pl.pallas_call(
        functools.partial(finish_kernel, base, aliased),
        in_specs=[kept_place] * len(carried) + [whole, whole],
        out_specs=[pl.BlockSpec(memory_space=pltpu.HBM)] * 2,
        out_shape=[jax.ShapeDtypeStruct(shape, jnp.bfloat16)] * 2,
        scratch_shapes=[
            pltpu.VMEM((2, shape[0], kept.shape[2]), jnp.bfloat16),
            pltpu.SemaphoreType.DMA((2,)),
        ],
        input_output_aliases={0: 0, 1: 1} if aliased else {},
        compiler_params=pltpu.CompilerParams(vmem_limit_bytes=SMALL_LIMIT),
        name="finish_keys_values",
    )(*carried, kept, returned)


def on_device(queries, keys, values, grad_out, episode_lengths):
    rows = queries.shape[0]
    groups = keys.shape[1] // HEAD_DIM
    count = lax.axis_size("seq")
    place = lax.axis_index("seq").astype(jnp.int32)
    odd = lax.bitwise_and(place, jnp.int32(1))
    first = jnp.reshape(place * rows, (1,))
    ahead = [(source, (source + 2) % count) for source in range(count)]
    behind = [((source + 2) % count, source) for source in range(count)]
    swap = [(source, source ^ 1) for source in range(count)]
    known = groups == sum(SENT)
    sent = SENT if known else (groups,)
    calls = CALLS if known else (groups,)
    returns = RETURNED if known else (groups,)
    starts = [sum(sent[:index]) for index in range(len(sent))]

    q_here, do_here, k_here, v_here = (in_hbm(x) for x in (queries, grad_out, keys, values))
    own = list(packed(k_here, v_here, [b * HEAD_DIM for b in starts], [s * HEAD_DIM for s in sent]))
    far = [permuted(block, ahead) for block in own]
    bias = masks(rows, episode_lengths, first)
    own[0], bias = lax.optimization_barrier((own[0], bias))
    near = [permuted(jnp.where(odd == 1, there, here), swap) for there, here in zip(far, own)]
    grads = None
    parts = []
    waiting = []
    stored = []
    skips = []
    base = begun = 0
    for size in calls:
        chunk = max(index for index, start in enumerate(starts) if start <= base)
        skips.append(base - starts[chunk])
        out, ds, back, kept = attention(
            base, size, skips[-1], queries.shape[1] // groups, first, bias, q_here, do_here, far[chunk], near[chunk], own[chunk]
        )
        stored.append((out, ds, far[chunk], near[chunk], own[chunk]))
        waiting.append((back, kept))
        base += size
        if base < begun + returns[len(parts)]:
            continue
        back = jnp.concatenate([pair[0] for pair in waiting], axis=3)
        kept = jnp.concatenate([pair[1] for pair in waiting], axis=2)
        waiting = []
        if parts:
            back, parts[-1][2] = lax.optimization_barrier((back, parts[-1][2]))
        beside = permuted(back[1], swap)
        none = jnp.zeros_like(beside)
        onward = back[0].astype(jnp.float32) + jnp.where(odd == 1, beside, none).astype(jnp.float32)
        kept = kept + jnp.where(odd == 1, none, beside).astype(jnp.float32)
        parts.append([begun, kept, permuted(onward.astype(jnp.bfloat16), behind)])
        begun = base
    attn_out, grad_queries = query_grads(calls, skips, queries.shape, stored)
    for begun, kept, returned in parts:
        grads = finished(begun, keys.shape, kept, returned, grads)
    return (attn_out, grad_queries, *grads)


def solution(mesh):
    split = P(("groups", "seq"), None)
    return jax.shard_map(
        on_device,
        mesh=mesh,
        in_specs=(split, split, split, split, P("groups")),
        out_specs=(split, split, split, split),
        check_vma=False,
    )
```

```python
import functools
import math

import jax
import jax.numpy as jnp
from jax import lax
from jax.experimental import pallas as pl
from jax.experimental.pallas import tpu as pltpu
from jax.sharding import PartitionSpec as P

HEAD_DIM = 128
TILE = 128
HEADS_AT_ONCE = 4
SENT = (2, 2)
CALLS = (2, 2)
RETURNED = (2, 2)
NT = (((1,), (1,)), ((), ()))
NN = (((1,), (0,)), ((), ()))
TN = (((0,), (0,)), ((), ()))
FACTOR = 1.0 / math.sqrt(HEAD_DIM)
FACTOR2 = math.log2(math.e) / math.sqrt(HEAD_DIM)
NEVER = -1e30
VMEM_LIMIT = 20 * 1024 * 1024
QUERY_LIMIT = 12 * 1024 * 1024
SMALL_LIMIT = 8 * 1024 * 1024


def matmul(left, right, dims):
    return lax.dot_general(left, right, dims, preferred_element_type=jnp.float32)


def permuted(value, pairs):
    return lax.ppermute(value, "seq", pairs)


def in_hbm(value):
    return pltpu.with_memory_space_constraint(value, pltpu.HBM)


def pack_kernel(starts, sizes, k_ref, v_ref, *outs):
    for out, start, size in zip(outs, starts, sizes):
        out[:, :size] = k_ref[:, start : start + size]
        out[:, size:] = v_ref[:, start : start + size]


def packed(keys, values, starts, sizes):
    rows = keys.shape[0]
    return pl.pallas_call(
        functools.partial(pack_kernel, starts, sizes),
        grid=(1,),
        in_specs=[pl.BlockSpec(keys.shape, lambda i: (0, 0))] * 2,
        out_specs=[pl.BlockSpec((rows, 2 * size), lambda i: (0, 0)) for size in sizes],
        out_shape=[jax.ShapeDtypeStruct((rows, 2 * size), keys.dtype) for size in sizes],
        compiler_params=pltpu.CompilerParams(vmem_limit_bytes=SMALL_LIMIT),
        name="pack_keys_values",
    )(keys, values)


def prepare_kernel(count, lengths_ref, first_ref, q_hbm, do_hbm, bias_ref, q_ref, do_ref, sems):
    fetches = [
        pltpu.make_async_copy(whole, held, sems.at[index])
        for index, (whole, held) in enumerate(((q_hbm, q_ref), (do_hbm, do_ref)))
    ]
    for fetch in fetches:
        fetch.start()
    tiles, _, band = bias_ref.shape
    rows = tiles * TILE
    row = lax.broadcasted_iota(jnp.int32, (rows, 1), 0)

    def one(index, carry):
        begin, start = carry
        return begin + lengths_ref[index], jnp.where(row >= begin, begin, start)

    _, start = lax.fori_loop(
        0, count, one, (-first_ref[0], jnp.full((rows, 1), -4 * rows, jnp.int32))
    )
    for tile in range(tiles):
        here = slice(tile * TILE, (tile + 1) * TILE)
        key = lax.broadcasted_iota(jnp.int32, (TILE, band), 1) + (tile * TILE - 2 * rows)
        allowed = (key >= start[here]) & (key <= row[here])
        bias_ref[tile] = jnp.where(allowed, 0.0, NEVER)
    for fetch in fetches:
        fetch.wait()


def prepared(lengths, first, q, do):
    rows = q.shape[0]
    smem = pl.BlockSpec(memory_space=pltpu.SMEM)
    far_away = pl.BlockSpec(memory_space=pltpu.HBM)
    whole = pl.BlockSpec(memory_space=pltpu.VMEM)
    return pl.pallas_call(
        functools.partial(prepare_kernel, lengths.shape[0]),
        in_specs=[smem, smem, far_away, far_away],
        out_specs=[whole] * 3,
        out_shape=[
            jax.ShapeDtypeStruct((rows // TILE, TILE, 2 * rows + TILE), jnp.float32),
            jax.ShapeDtypeStruct(q.shape, q.dtype),
            jax.ShapeDtypeStruct(do.shape, do.dtype),
        ],
        scratch_shapes=[pltpu.SemaphoreType.DMA((2,))],
        compiler_params=pltpu.CompilerParams(vmem_limit_bytes=SMALL_LIMIT),
        name="prepare",
    )(lengths, first, q, do)


def lanes(block, width=HEAD_DIM):
    return pl.ds(pl.multiple_of(block * width, width), width)


def attention_kernel(base, skipped, first_ref, bias, q_ref, do_ref, far, near, own, *refs):
    o_ref, ds_ref, back_ref, own_ref, k_all, v_all, dk_sum, dv_sum = refs
    group = pl.program_id(0)
    groups, tiles, _, _ = ds_ref.shape
    rows = far.shape[0]
    sent = far.shape[1] // (2 * HEAD_DIM)
    wide = o_ref.shape[2]
    heads = wide // HEAD_DIM
    per_call = min(HEADS_AT_ONCE, heads)
    k_col = lanes(skipped + group)
    v_col = lanes(sent + skipped + group)
    for place, part in enumerate((far, near, own)):
        k_all[place * rows : (place + 1) * rows] = part[:, k_col]
        v_all[place * rows : (place + 1) * rows] = part[:, v_col]

    def all_units(lowest):
        dk_sum[...] = jnp.zeros_like(dk_sum)
        dv_sum[...] = jnp.zeros_like(dv_sum)
        units = [(tile, first) for tile in range(tiles) for first in range(0, heads, per_call)]

        def places(unit):
            tile, first = unit
            here = slice(tile * TILE, (tile + 1) * TILE)
            keys = slice(max(tile * TILE, lowest), tile * TILE + 2 * rows + TILE)
            cols = [slice((first + x) * HEAD_DIM, (first + x + 1) * HEAD_DIM) for x in range(per_call)]
            return here, keys, cols

        def stacked(ref, unit):
            here, _, cols = places(unit)
            first = (base + group) * heads
            return jnp.concatenate([ref[here, lanes(first + c.start // HEAD_DIM)] for c in cols], 0)

        def scores(unit):
            return matmul(stacked(q_ref, unit), k_all[places(unit)[1]], NT)

        def softmax(unit, s):
            _, keys, _ = places(unit)
            width = keys.stop - keys.start
            shut = bias[unit[0], :, keys.start - unit[0] * TILE :]
            s = s.reshape(per_call, TILE, width) * FACTOR2 + shut[None]
            s = s.reshape(per_call * TILE, width)
            e = jnp.exp2(s - jnp.max(s, 1, keepdims=True))
            return e * (1.0 / jnp.sum(e, 1, keepdims=True))

        def score_grads(unit, prob, weight):
            here, keys, cols = places(unit)
            do = stacked(do_ref, unit)
            out = matmul(weight, v_all[keys], NN).astype(jnp.bfloat16)
            for x, c in enumerate(cols):
                o_ref[group, here, c] = out[x * TILE : (x + 1) * TILE]
            dp = matmul(do, v_all[keys], NT)
            delta = jnp.sum(out.astype(jnp.float32) * do.astype(jnp.float32), 1, keepdims=True)
            ds = (prob * (dp - delta)).astype(jnp.bfloat16)
            tile, first = unit
            ds_ref[group, tile, first * TILE : (first + per_call) * TILE, keys.start - tile * TILE :] = ds
            return ds

        def sums(unit, weight, ds):
            _, keys, _ = places(unit)
            dv_sum[:, keys] += matmul(stacked(do_ref, unit), weight, TN)
            dk_sum[:, keys] += matmul(stacked(q_ref, unit), ds, TN)

        ahead = scores(units[0])
        before = None
        for index, unit in enumerate(units):
            now = ahead
            if index + 1 < len(units):
                ahead = scores(units[index + 1])
            prob = softmax(unit, now)
            weight = prob.astype(jnp.bfloat16)
            if before is not None:
                sums(*before)
            before = (unit, weight, score_grads(unit, prob, weight))
        sums(*before)
        if lowest:
            for tile in range(tiles):
                gap = max(0, lowest - tile * TILE)
                ds_ref[group, tile, :, :gap] = jnp.zeros((heads * TILE, gap), jnp.bfloat16)

        here = lanes(group)
        own_ref[0, :, here] = dk_sum[:, 2 * rows :].T * FACTOR
        own_ref[1, :, here] = dv_sum[:, 2 * rows :].T
        for place in range(2):
            span = slice(place * rows, (place + 1) * rows)
            back_ref[place, 0, :, here] = (dk_sum[:, span].T * FACTOR).astype(jnp.bfloat16)
            back_ref[place, 1, :, here] = dv_sum[:, span].T.astype(jnp.bfloat16)

    @pl.when(first_ref[0] >= 2 * rows)
    def _():
        all_units(0)

    @pl.when(first_ref[0] < 2 * rows)
    def _():
        all_units(rows)


def attention(base, groups, skipped, head_cols, first, bias, q, do, far, near, own):
    rows = q.shape[0]
    tiles, _, band = bias.shape
    whole = pl.BlockSpec(memory_space=pltpu.VMEM)
    return pl.pallas_call(
        functools.partial(attention_kernel, base, skipped),
        grid=(groups,),
        in_specs=[pl.BlockSpec(memory_space=pltpu.SMEM), whole, whole, whole, whole, whole, whole],
        out_specs=[whole] * 4,
        out_shape=[
            jax.ShapeDtypeStruct((groups, rows, head_cols), jnp.bfloat16),
            jax.ShapeDtypeStruct((groups, tiles, head_cols // HEAD_DIM * TILE, band), jnp.bfloat16),
            jax.ShapeDtypeStruct((2, 2, rows, groups * HEAD_DIM), jnp.bfloat16),
            jax.ShapeDtypeStruct((2, rows, groups * HEAD_DIM), jnp.float32),
        ],
        scratch_shapes=[
            pltpu.VMEM((3 * rows, HEAD_DIM), jnp.bfloat16),
            pltpu.VMEM((3 * rows, HEAD_DIM), jnp.bfloat16),
            pltpu.VMEM((HEAD_DIM, 3 * rows), jnp.float32),
            pltpu.VMEM((HEAD_DIM, 3 * rows), jnp.float32),
        ],
        compiler_params=pltpu.CompilerParams(vmem_limit_bytes=VMEM_LIMIT),
        name="attention",
    )(first, bias, q, do, far, near, own)


def query_kernel(calls, skips, *refs):
    o_out, dq_out, k_all, held, sems = refs[-5:]
    rows = held.shape[0]
    wide = held.shape[1] // sum(calls)
    groups = [(index, here) for index, size in enumerate(calls) for here in range(size)]
    copies = []
    for place, (index, here) in enumerate(groups):
        cols = pl.ds(place * wide, wide)
        copies.append(pltpu.make_async_copy(refs[5 * index].at[here], o_out.at[:, cols], sems.at[place, 0]))
        copies[-1].start()
    for place, (index, here) in enumerate(groups):
        _, ds_ref, *parts = refs[5 * index : 5 * index + 5]
        column = slice((skips[index] + here) * HEAD_DIM, (skips[index] + here + 1) * HEAD_DIM)
        for spot, part in enumerate(parts):
            k_all[spot * rows : (spot + 1) * rows] = part[:, column]
        for tile in range(ds_ref.shape[1]):
            k = k_all[tile * TILE : tile * TILE + ds_ref.shape[3]]
            dq = (matmul(ds_ref[here, tile], k, NN) * FACTOR).astype(jnp.bfloat16)
            for x in range(wide // HEAD_DIM):
                start = place * wide + x * HEAD_DIM
                held[tile * TILE : (tile + 1) * TILE, start : start + HEAD_DIM] = dq[x * TILE : (x + 1) * TILE]
        cols = pl.ds(place * wide, wide)
        copies.append(pltpu.make_async_copy(held.at[:, cols], dq_out.at[:, cols], sems.at[place, 1]))
        copies[-1].start()
    for copy in copies:
        copy.wait()


def query_grads(calls, skips, shape, parts):
    rows, width = shape
    flat = [array for part in parts for array in part]
    return pl.pallas_call(
        functools.partial(query_kernel, calls, skips),
        in_specs=[pl.BlockSpec(memory_space=pltpu.VMEM)] * len(flat),
        out_specs=[pl.BlockSpec(memory_space=pltpu.HBM)] * 2,
        out_shape=[jax.ShapeDtypeStruct(shape, jnp.bfloat16)] * 2,
        scratch_shapes=[
            pltpu.VMEM((3 * rows, HEAD_DIM), jnp.bfloat16),
            pltpu.VMEM(shape, jnp.bfloat16),
            pltpu.SemaphoreType.DMA((sum(calls), 2)),
        ],
        compiler_params=pltpu.CompilerParams(vmem_limit_bytes=QUERY_LIMIT),
        name="query_grads",
    )(*flat)


def finish_kernel(base, aliased, *refs):
    refs = refs[2:] if aliased else refs
    kept_ref, returned_ref, gk_ref, gv_ref, total, sems = refs
    span = pl.ds(base * HEAD_DIM, kept_ref.shape[2])
    copies = []
    for index, out in enumerate((gk_ref, gv_ref)):
        total[index] = (kept_ref[index] + returned_ref[index].astype(jnp.float32)).astype(jnp.bfloat16)
        copies.append(pltpu.make_async_copy(total.at[index], out.at[:, span], sems.at[index]))
        copies[-1].start()
    for copy in copies:
        copy.wait()


def finished(base, shape, kept, returned, carried):
    aliased = carried is not None
    carried = carried if aliased else ()
    kept_place = pl.BlockSpec(memory_space=pl.ANY)
    whole = pl.BlockSpec(memory_space=pltpu.VMEM)
    return pl.pallas_call(
        functools.partial(finish_kernel, base, aliased),
        in_specs=[kept_place] * len(carried) + [whole, whole],
        out_specs=[pl.BlockSpec(memory_space=pltpu.HBM)] * 2,
        out_shape=[jax.ShapeDtypeStruct(shape, jnp.bfloat16)] * 2,
        scratch_shapes=[
            pltpu.VMEM((2, shape[0], kept.shape[2]), jnp.bfloat16),
            pltpu.SemaphoreType.DMA((2,)),
        ],
        input_output_aliases={0: 0, 1: 1} if aliased else {},
        compiler_params=pltpu.CompilerParams(vmem_limit_bytes=SMALL_LIMIT),
        name="finish_keys_values",
    )(*carried, kept, returned)


def on_device(queries, keys, values, grad_out, episode_lengths):
    rows = queries.shape[0]
    groups = keys.shape[1] // HEAD_DIM
    count = lax.axis_size("seq")
    place = lax.axis_index("seq").astype(jnp.int32)
    odd = lax.bitwise_and(place, jnp.int32(1))
    first = jnp.reshape(place * rows, (1,))
    ahead = [(source, (source + 2) % count) for source in range(count)]
    behind = [((source + 2) % count, source) for source in range(count)]
    swap = [(source, source ^ 1) for source in range(count)]
    known = groups == sum(SENT)
    sent = SENT if known else (groups,)
    calls = CALLS if known else (groups,)
    returns = RETURNED if known else (groups,)
    starts = [sum(sent[:index]) for index in range(len(sent))]

    q_here, do_here, k_here, v_here = (in_hbm(x) for x in (queries, grad_out, keys, values))
    own = list(packed(k_here, v_here, [b * HEAD_DIM for b in starts], [s * HEAD_DIM for s in sent]))
    far = [permuted(block, ahead) for block in own]
    bias, q_here, do_here = prepared(episode_lengths, first, q_here, do_here)
    own[0], bias = lax.optimization_barrier((own[0], bias))
    near = [permuted(jnp.where(odd == 1, there, here), swap) for there, here in zip(far, own)]
    grads = None
    parts = []
    waiting = []
    stored = []
    skips = []
    base = begun = 0
    for size in calls:
        chunk = max(index for index, start in enumerate(starts) if start <= base)
        skips.append(base - starts[chunk])
        out, ds, back, kept = attention(
            base, size, skips[-1], queries.shape[1] // groups, first, bias, q_here, do_here, far[chunk], near[chunk], own[chunk]
        )
        stored.append((out, ds, far[chunk], near[chunk], own[chunk]))
        waiting.append((back, kept))
        base += size
        if base < begun + returns[len(parts)]:
            continue
        back = jnp.concatenate([pair[0] for pair in waiting], axis=3)
        kept = jnp.concatenate([pair[1] for pair in waiting], axis=2)
        waiting = []
        if parts:
            back, parts[-1][2] = lax.optimization_barrier((back, parts[-1][2]))
        beside = permuted(back[1], swap)
        none = jnp.zeros_like(beside)
        onward = back[0].astype(jnp.float32) + jnp.where(odd == 1, beside, none).astype(jnp.float32)
        kept = kept + jnp.where(odd == 1, none, beside).astype(jnp.float32)
        parts.append([begun, kept, permuted(onward.astype(jnp.bfloat16), behind)])
        begun = base
    attn_out, grad_queries = query_grads(calls, skips, queries.shape, stored)
    for begun, kept, returned in parts:
        grads = finished(begun, keys.shape, kept, returned, grads)
    return (attn_out, grad_queries, *grads)


def solution(mesh):
    split = P(("groups", "seq"), None)
    return jax.shard_map(
        on_device,
        mesh=mesh,
        in_specs=(split, split, split, split, P("groups")),
        out_specs=(split, split, split, split),
        check_vma=False,
    )
```

```python
import functools
import math

import jax
import jax.numpy as jnp
from jax import lax
from jax.experimental import pallas as pl
from jax.experimental.pallas import tpu as pltpu
from jax.sharding import PartitionSpec as P

HEAD_DIM = 128
TILE = 128
HEADS_AT_ONCE = 4
SENT = (1, 3)
CALLS = (1, 3)
RETURNED = (1, 3)
NT = (((1,), (1,)), ((), ()))
NN = (((1,), (0,)), ((), ()))
TN = (((0,), (0,)), ((), ()))
FACTOR = 1.0 / math.sqrt(HEAD_DIM)
FACTOR2 = math.log2(math.e) / math.sqrt(HEAD_DIM)
NEVER = -1e30
VMEM_LIMIT = 20 * 1024 * 1024
QUERY_LIMIT = 12 * 1024 * 1024
SMALL_LIMIT = 8 * 1024 * 1024


def matmul(left, right, dims):
    return lax.dot_general(left, right, dims, preferred_element_type=jnp.float32)


def permuted(value, pairs):
    return lax.ppermute(value, "seq", pairs)


def in_hbm(value):
    return pltpu.with_memory_space_constraint(value, pltpu.HBM)


def pack_kernel(starts, sizes, k_hbm, v_hbm, *refs):
    outs, sems = refs[:-1], refs[-1]
    copies = []
    for index, (start, size) in enumerate(zip(starts, sizes)):
        for place, whole in enumerate((k_hbm, v_hbm)):
            held = outs[index].at[:, pl.ds(place * size, size)]
            copies.append(pltpu.make_async_copy(whole.at[:, pl.ds(start, size)], held, sems.at[index, place]))
            copies[-1].start()
    for copy in copies:
        copy.wait()


def packed(keys, values, starts, sizes):
    rows = keys.shape[0]
    return pl.pallas_call(
        functools.partial(pack_kernel, starts, sizes),
        in_specs=[pl.BlockSpec(memory_space=pltpu.HBM)] * 2,
        out_specs=[pl.BlockSpec(memory_space=pltpu.VMEM)] * len(sizes),
        out_shape=[jax.ShapeDtypeStruct((rows, 2 * size), keys.dtype) for size in sizes],
        scratch_shapes=[pltpu.SemaphoreType.DMA((len(sizes), 2))],
        compiler_params=pltpu.CompilerParams(vmem_limit_bytes=SMALL_LIMIT),
        name="pack_keys_values",
    )(keys, values)


def prepare_kernel(count, lengths_ref, first_ref, q_hbm, do_hbm, bias_ref, q_ref, do_ref, sems):
    fetches = [
        pltpu.make_async_copy(whole, held, sems.at[index])
        for index, (whole, held) in enumerate(((q_hbm, q_ref), (do_hbm, do_ref)))
    ]
    for fetch in fetches:
        fetch.start()
    tiles, _, band = bias_ref.shape
    rows = tiles * TILE
    row = lax.broadcasted_iota(jnp.int32, (rows, 1), 0)

    def one(index, carry):
        begin, start = carry
        return begin + lengths_ref[index], jnp.where(row >= begin, begin, start)

    _, start = lax.fori_loop(
        0, count, one, (-first_ref[0], jnp.full((rows, 1), -4 * rows, jnp.int32))
    )
    for tile in range(tiles):
        here = slice(tile * TILE, (tile + 1) * TILE)
        key = lax.broadcasted_iota(jnp.int32, (TILE, band), 1) + (tile * TILE - 2 * rows)
        allowed = (key >= start[here]) & (key <= row[here])
        bias_ref[tile] = jnp.where(allowed, 0.0, NEVER)
    for fetch in fetches:
        fetch.wait()


def prepared(lengths, first, q, do):
    rows = q.shape[0]
    smem = pl.BlockSpec(memory_space=pltpu.SMEM)
    far_away = pl.BlockSpec(memory_space=pltpu.HBM)
    whole = pl.BlockSpec(memory_space=pltpu.VMEM)
    return pl.pallas_call(
        functools.partial(prepare_kernel, lengths.shape[0]),
        in_specs=[smem, smem, far_away, far_away],
        out_specs=[whole] * 3,
        out_shape=[
            jax.ShapeDtypeStruct((rows // TILE, TILE, 2 * rows + TILE), jnp.float32),
            jax.ShapeDtypeStruct(q.shape, q.dtype),
            jax.ShapeDtypeStruct(do.shape, do.dtype),
        ],
        scratch_shapes=[pltpu.SemaphoreType.DMA((2,))],
        compiler_params=pltpu.CompilerParams(vmem_limit_bytes=SMALL_LIMIT),
        name="prepare",
    )(lengths, first, q, do)


def lanes(block, width=HEAD_DIM):
    return pl.ds(pl.multiple_of(block * width, width), width)


def attention_kernel(base, skipped, first_ref, bias, q_ref, do_ref, far, near, own, *refs):
    o_ref, ds_ref, back_ref, own_ref, k_all, v_all, dk_sum, dv_sum = refs
    group = pl.program_id(0)
    groups, tiles, _, _ = ds_ref.shape
    rows = far.shape[0]
    sent = far.shape[1] // (2 * HEAD_DIM)
    wide = o_ref.shape[2]
    heads = wide // HEAD_DIM
    per_call = min(HEADS_AT_ONCE, heads)
    k_col = lanes(skipped + group)
    v_col = lanes(sent + skipped + group)
    for place, part in enumerate((far, near, own)):
        k_all[place * rows : (place + 1) * rows] = part[:, k_col]
        v_all[place * rows : (place + 1) * rows] = part[:, v_col]

    def all_units(lowest):
        dk_sum[...] = jnp.zeros_like(dk_sum)
        dv_sum[...] = jnp.zeros_like(dv_sum)
        units = [(tile, first) for tile in range(tiles) for first in range(0, heads, per_call)]

        def places(unit):
            tile, first = unit
            here = slice(tile * TILE, (tile + 1) * TILE)
            keys = slice(max(tile * TILE, lowest), tile * TILE + 2 * rows + TILE)
            cols = [slice((first + x) * HEAD_DIM, (first + x + 1) * HEAD_DIM) for x in range(per_call)]
            return here, keys, cols

        def stacked(ref, unit):
            here, _, cols = places(unit)
            first = (base + group) * heads
            return jnp.concatenate([ref[here, lanes(first + c.start // HEAD_DIM)] for c in cols], 0)

        def scores(unit):
            return matmul(stacked(q_ref, unit), k_all[places(unit)[1]], NT)

        def softmax(unit, s):
            _, keys, _ = places(unit)
            width = keys.stop - keys.start
            shut = bias[unit[0], :, keys.start - unit[0] * TILE :]
            s = s.reshape(per_call, TILE, width) * FACTOR2 + shut[None]
            s = s.reshape(per_call * TILE, width)
            e = jnp.exp2(s - jnp.max(s, 1, keepdims=True))
            return e * (1.0 / jnp.sum(e, 1, keepdims=True))

        def score_grads(unit, weight):
            here, keys, cols = places(unit)
            do = stacked(do_ref, unit)
            out = matmul(weight, v_all[keys], NN).astype(jnp.bfloat16)
            for x, c in enumerate(cols):
                o_ref[group, here, c] = out[x * TILE : (x + 1) * TILE]
            dp = matmul(do, v_all[keys], NT)
            delta = jnp.sum(out.astype(jnp.float32) * do.astype(jnp.float32), 1, keepdims=True)
            ds = weight * (dp - delta).astype(jnp.bfloat16)
            tile, first = unit
            ds_ref[group, tile, first * TILE : (first + per_call) * TILE, keys.start - tile * TILE :] = ds
            return ds

        def sums(unit, weight, ds):
            _, keys, _ = places(unit)
            dv_sum[:, keys] += matmul(stacked(do_ref, unit), weight, TN)
            dk_sum[:, keys] += matmul(stacked(q_ref, unit), ds, TN)

        ahead = scores(units[0])
        before = None
        for index, unit in enumerate(units):
            now = ahead
            if index + 1 < len(units):
                ahead = scores(units[index + 1])
            weight = softmax(unit, now).astype(jnp.bfloat16)
            if before is not None:
                sums(*before)
            before = (unit, weight, score_grads(unit, weight))
        sums(*before)
        if lowest:
            for tile in range(tiles):
                gap = max(0, lowest - tile * TILE)
                ds_ref[group, tile, :, :gap] = jnp.zeros((heads * TILE, gap), jnp.bfloat16)

        here = lanes(group)
        own_ref[0, :, here] = dk_sum[:, 2 * rows :].T * FACTOR
        own_ref[1, :, here] = dv_sum[:, 2 * rows :].T
        for place in range(2):
            span = slice(place * rows, (place + 1) * rows)
            back_ref[place, 0, :, here] = (dk_sum[:, span].T * FACTOR).astype(jnp.bfloat16)
            back_ref[place, 1, :, here] = dv_sum[:, span].T.astype(jnp.bfloat16)

    @pl.when(first_ref[0] >= 2 * rows)
    def _():
        all_units(0)

    @pl.when(first_ref[0] < 2 * rows)
    def _():
        all_units(rows)


def attention(base, groups, skipped, head_cols, first, bias, q, do, far, near, own):
    rows = q.shape[0]
    tiles, _, band = bias.shape
    whole = pl.BlockSpec(memory_space=pltpu.VMEM)
    return pl.pallas_call(
        functools.partial(attention_kernel, base, skipped),
        grid=(groups,),
        in_specs=[pl.BlockSpec(memory_space=pltpu.SMEM), whole, whole, whole, whole, whole, whole],
        out_specs=[whole] * 4,
        out_shape=[
            jax.ShapeDtypeStruct((groups, rows, head_cols), jnp.bfloat16),
            jax.ShapeDtypeStruct((groups, tiles, head_cols // HEAD_DIM * TILE, band), jnp.bfloat16),
            jax.ShapeDtypeStruct((2, 2, rows, groups * HEAD_DIM), jnp.bfloat16),
            jax.ShapeDtypeStruct((2, rows, groups * HEAD_DIM), jnp.float32),
        ],
        scratch_shapes=[
            pltpu.VMEM((3 * rows, HEAD_DIM), jnp.bfloat16),
            pltpu.VMEM((3 * rows, HEAD_DIM), jnp.bfloat16),
            pltpu.VMEM((HEAD_DIM, 3 * rows), jnp.float32),
            pltpu.VMEM((HEAD_DIM, 3 * rows), jnp.float32),
        ],
        compiler_params=pltpu.CompilerParams(vmem_limit_bytes=VMEM_LIMIT),
        name="attention",
    )(first, bias, q, do, far, near, own)


def query_kernel(calls, skips, *refs):
    o_out, dq_out, k_all, held, sems = refs[-5:]
    rows = held.shape[0]
    wide = held.shape[1] // sum(calls)
    groups = [(index, here) for index, size in enumerate(calls) for here in range(size)]
    copies = []
    for place, (index, here) in enumerate(groups):
        cols = pl.ds(place * wide, wide)
        copies.append(pltpu.make_async_copy(refs[5 * index].at[here], o_out.at[:, cols], sems.at[place, 0]))
        copies[-1].start()
    for place, (index, here) in enumerate(groups):
        _, ds_ref, *parts = refs[5 * index : 5 * index + 5]
        column = slice((skips[index] + here) * HEAD_DIM, (skips[index] + here + 1) * HEAD_DIM)
        for spot, part in enumerate(parts):
            k_all[spot * rows : (spot + 1) * rows] = part[:, column]
        for tile in range(ds_ref.shape[1]):
            k = k_all[tile * TILE : tile * TILE + ds_ref.shape[3]]
            dq = (matmul(ds_ref[here, tile], k, NN) * FACTOR).astype(jnp.bfloat16)
            for x in range(wide // HEAD_DIM):
                start = place * wide + x * HEAD_DIM
                held[tile * TILE : (tile + 1) * TILE, start : start + HEAD_DIM] = dq[x * TILE : (x + 1) * TILE]
        cols = pl.ds(place * wide, wide)
        copies.append(pltpu.make_async_copy(held.at[:, cols], dq_out.at[:, cols], sems.at[place, 1]))
        copies[-1].start()
    for copy in copies:
        copy.wait()


def query_grads(calls, skips, shape, parts):
    rows, width = shape
    flat = [array for part in parts for array in part]
    return pl.pallas_call(
        functools.partial(query_kernel, calls, skips),
        in_specs=[pl.BlockSpec(memory_space=pltpu.VMEM)] * len(flat),
        out_specs=[pl.BlockSpec(memory_space=pltpu.HBM)] * 2,
        out_shape=[jax.ShapeDtypeStruct(shape, jnp.bfloat16)] * 2,
        scratch_shapes=[
            pltpu.VMEM((3 * rows, HEAD_DIM), jnp.bfloat16),
            pltpu.VMEM(shape, jnp.bfloat16),
            pltpu.SemaphoreType.DMA((sum(calls), 2)),
        ],
        compiler_params=pltpu.CompilerParams(vmem_limit_bytes=QUERY_LIMIT),
        name="query_grads",
    )(*flat)


def finish_kernel(base, aliased, *refs):
    refs = refs[2:] if aliased else refs
    kept_ref, returned_ref, gk_ref, gv_ref, total, sems = refs
    span = pl.ds(base * HEAD_DIM, kept_ref.shape[2])
    copies = []
    for index, out in enumerate((gk_ref, gv_ref)):
        total[index] = (kept_ref[index] + returned_ref[index].astype(jnp.float32)).astype(jnp.bfloat16)
        copies.append(pltpu.make_async_copy(total.at[index], out.at[:, span], sems.at[index]))
        copies[-1].start()
    for copy in copies:
        copy.wait()


def finished(base, shape, kept, returned, carried):
    aliased = carried is not None
    carried = carried if aliased else ()
    kept_place = pl.BlockSpec(memory_space=pl.ANY)
    whole = pl.BlockSpec(memory_space=pltpu.VMEM)
    return pl.pallas_call(
        functools.partial(finish_kernel, base, aliased),
        in_specs=[kept_place] * len(carried) + [whole, whole],
        out_specs=[pl.BlockSpec(memory_space=pltpu.HBM)] * 2,
        out_shape=[jax.ShapeDtypeStruct(shape, jnp.bfloat16)] * 2,
        scratch_shapes=[
            pltpu.VMEM((2, shape[0], kept.shape[2]), jnp.bfloat16),
            pltpu.SemaphoreType.DMA((2,)),
        ],
        input_output_aliases={0: 0, 1: 1} if aliased else {},
        compiler_params=pltpu.CompilerParams(vmem_limit_bytes=SMALL_LIMIT),
        name="finish_keys_values",
    )(*carried, kept, returned)


def on_device(queries, keys, values, grad_out, episode_lengths):
    rows = queries.shape[0]
    groups = keys.shape[1] // HEAD_DIM
    count = lax.axis_size("seq")
    place = lax.axis_index("seq").astype(jnp.int32)
    odd = lax.bitwise_and(place, jnp.int32(1))
    first = jnp.reshape(place * rows, (1,))
    ahead = [(source, (source + 2) % count) for source in range(count)]
    behind = [((source + 2) % count, source) for source in range(count)]
    swap = [(source, source ^ 1) for source in range(count)]
    known = groups == sum(SENT)
    sent = SENT if known else (groups,)
    calls = CALLS if known else (groups,)
    returns = RETURNED if known else (groups,)
    starts = [sum(sent[:index]) for index in range(len(sent))]

    q_here, do_here, k_here, v_here = (in_hbm(x) for x in (queries, grad_out, keys, values))
    own = list(packed(k_here, v_here, [start * HEAD_DIM for start in starts], [size * HEAD_DIM for size in sent]))
    far = [permuted(block, ahead) for block in own]
    bias, q_here, do_here = prepared(episode_lengths, first, q_here, do_here)
    own[0], bias = lax.optimization_barrier((own[0], bias))
    near = [permuted(jnp.where(odd == 1, there, here), swap) for there, here in zip(far, own)]
    grads = None
    parts = []
    waiting = []
    stored = []
    skips = []
    base = begun = 0
    for size in calls:
        chunk = max(index for index, start in enumerate(starts) if start <= base)
        skips.append(base - starts[chunk])
        out, ds, back, kept = attention(
            base, size, skips[-1], queries.shape[1] // groups, first, bias, q_here, do_here, far[chunk], near[chunk], own[chunk]
        )
        stored.append((out, ds, far[chunk], near[chunk], own[chunk]))
        waiting.append((back, kept))
        base += size
        if base < begun + returns[len(parts)]:
            continue
        back = jnp.concatenate([pair[0] for pair in waiting], axis=3)
        kept = jnp.concatenate([pair[1] for pair in waiting], axis=2)
        waiting = []
        if parts:
            back, parts[-1][2] = lax.optimization_barrier((back, parts[-1][2]))
        beside = permuted(back[1], swap)
        none = jnp.zeros_like(beside)
        onward = back[0].astype(jnp.float32) + jnp.where(odd == 1, beside, none).astype(jnp.float32)
        kept = kept + jnp.where(odd == 1, none, beside).astype(jnp.float32)
        parts.append([begun, kept, permuted(onward.astype(jnp.bfloat16), behind)])
        begun = base
    attn_out, grad_queries = query_grads(calls, skips, queries.shape, stored)
    for begun, kept, returned in parts:
        grads = finished(begun, keys.shape, kept, returned, grads)
    return (attn_out, grad_queries, *grads)


def solution(mesh):
    split = P(("groups", "seq"), None)
    return jax.shard_map(
        on_device,
        mesh=mesh,
        in_specs=(split, split, split, split, P("groups")),
        out_specs=(split, split, split, split),
        check_vma=False,
    )
```

```python
import functools
import math

import jax
import jax.numpy as jnp
from jax import lax
from jax.experimental import pallas as pl
from jax.experimental.pallas import tpu as pltpu
from jax.sharding import PartitionSpec as P

HEAD_DIM = 128
TILE = 128
HEADS_AT_ONCE = 4
SENT = (1, 3)
CALLS = (1, 3)
RETURNED = (1, 3)
NT = (((1,), (1,)), ((), ()))
NN = (((1,), (0,)), ((), ()))
TN = (((0,), (0,)), ((), ()))
FACTOR = 1.0 / math.sqrt(HEAD_DIM)
FACTOR2 = math.log2(math.e) / math.sqrt(HEAD_DIM)
NEVER = -1e30
VMEM_LIMIT = 20 * 1024 * 1024
QUERY_LIMIT = 12 * 1024 * 1024
SMALL_LIMIT = 8 * 1024 * 1024


def matmul(left, right, dims):
    return lax.dot_general(left, right, dims, preferred_element_type=jnp.float32)


def permuted(value, pairs):
    return lax.ppermute(value, "seq", pairs)


def in_hbm(value):
    return pltpu.with_memory_space_constraint(value, pltpu.HBM)


def pack_kernel(starts, sizes, k_hbm, v_hbm, *refs):
    outs, sems = refs[:-1], refs[-1]
    copies = []
    for index, (start, size) in enumerate(zip(starts, sizes)):
        for place, whole in enumerate((k_hbm, v_hbm)):
            held = outs[index].at[:, pl.ds(place * size, size)]
            copies.append(pltpu.make_async_copy(whole.at[:, pl.ds(start, size)], held, sems.at[index, place]))
            copies[-1].start()
    for copy in copies:
        copy.wait()


def packed(keys, values, starts, sizes):
    rows = keys.shape[0]
    return pl.pallas_call(
        functools.partial(pack_kernel, starts, sizes),
        in_specs=[pl.BlockSpec(memory_space=pltpu.HBM)] * 2,
        out_specs=[pl.BlockSpec(memory_space=pltpu.VMEM)] * len(sizes),
        out_shape=[jax.ShapeDtypeStruct((rows, 2 * size), keys.dtype) for size in sizes],
        scratch_shapes=[pltpu.SemaphoreType.DMA((len(sizes), 2))],
        compiler_params=pltpu.CompilerParams(vmem_limit_bytes=SMALL_LIMIT),
        name="pack_keys_values",
    )(keys, values)


def prepare_kernel(count, lengths_ref, first_ref, q_hbm, do_hbm, bias_ref, q_ref, do_ref, sems):
    span = pl.ds(0, q_ref.shape[1])
    fetches = [
        pltpu.make_async_copy(whole.at[:, span], held, sems.at[index])
        for index, (whole, held) in enumerate(((q_hbm, q_ref), (do_hbm, do_ref)))
    ]
    for fetch in fetches:
        fetch.start()
    tiles, _, band = bias_ref.shape
    rows = tiles * TILE
    row = lax.broadcasted_iota(jnp.int32, (rows, 1), 0)

    def one(index, carry):
        begin, start = carry
        return begin + lengths_ref[index], jnp.where(row >= begin, begin, start)

    _, start = lax.fori_loop(
        0, count, one, (-first_ref[0], jnp.full((rows, 1), -4 * rows, jnp.int32))
    )
    for tile in range(tiles):
        here = slice(tile * TILE, (tile + 1) * TILE)
        key = lax.broadcasted_iota(jnp.int32, (TILE, band), 1) + (tile * TILE - 2 * rows)
        allowed = (key >= start[here]) & (key <= row[here])
        bias_ref[tile] = jnp.where(allowed, 0.0, NEVER)
    for fetch in fetches:
        fetch.wait()


def prepared(lengths, first, q, do, width):
    rows = q.shape[0]
    smem = pl.BlockSpec(memory_space=pltpu.SMEM)
    far_away = pl.BlockSpec(memory_space=pltpu.HBM)
    whole = pl.BlockSpec(memory_space=pltpu.VMEM)
    return pl.pallas_call(
        functools.partial(prepare_kernel, lengths.shape[0]),
        in_specs=[smem, smem, far_away, far_away],
        out_specs=[whole] * 3,
        out_shape=[
            jax.ShapeDtypeStruct((rows // TILE, TILE, 2 * rows + TILE), jnp.float32),
            jax.ShapeDtypeStruct((rows, width), q.dtype),
            jax.ShapeDtypeStruct((rows, width), do.dtype),
        ],
        scratch_shapes=[pltpu.SemaphoreType.DMA((2,))],
        compiler_params=pltpu.CompilerParams(vmem_limit_bytes=SMALL_LIMIT),
        name="prepare",
    )(lengths, first, q, do)


def lanes(block, width=HEAD_DIM):
    return pl.ds(pl.multiple_of(block * width, width), width)


def attention_kernel(base, skipped, fetching, first_ref, bias, q_ref, do_ref, far, near, own, *refs):
    fetches = []
    if fetching:
        q_hbm, do_hbm, *refs, sems = refs
        q_rest, do_rest = refs[4:6]
        refs = refs[:4] + refs[6:]
        span = pl.ds(q_ref.shape[1], q_rest.shape[1])
        for index, (whole, held) in enumerate(((q_hbm, q_rest), (do_hbm, do_rest))):
            fetches.append(pltpu.make_async_copy(whole.at[:, span], held, sems.at[index]))
    o_ref, ds_ref, back_ref, own_ref, k_all, v_all, dk_sum, dv_sum = refs
    group = pl.program_id(0)
    groups, tiles, _, _ = ds_ref.shape
    rows = far.shape[0]
    sent = far.shape[1] // (2 * HEAD_DIM)
    wide = o_ref.shape[2]
    heads = wide // HEAD_DIM
    per_call = min(HEADS_AT_ONCE, heads)
    @pl.when(group == 0)
    def _():
        for fetch in fetches:
            fetch.start()

    k_col = lanes(skipped + group)
    v_col = lanes(sent + skipped + group)
    for place, part in enumerate((far, near, own)):
        k_all[place * rows : (place + 1) * rows] = part[:, k_col]
        v_all[place * rows : (place + 1) * rows] = part[:, v_col]

    def all_units(lowest):
        dk_sum[...] = jnp.zeros_like(dk_sum)
        dv_sum[...] = jnp.zeros_like(dv_sum)
        units = [(tile, first) for tile in range(tiles) for first in range(0, heads, per_call)]

        def places(unit):
            tile, first = unit
            here = slice(tile * TILE, (tile + 1) * TILE)
            keys = slice(max(tile * TILE, lowest), tile * TILE + 2 * rows + TILE)
            cols = [slice((first + x) * HEAD_DIM, (first + x + 1) * HEAD_DIM) for x in range(per_call)]
            return here, keys, cols

        def stacked(ref, unit):
            here, _, cols = places(unit)
            first = (base + group) * heads
            return jnp.concatenate([ref[here, lanes(first + c.start // HEAD_DIM)] for c in cols], 0)

        def scores(unit):
            return matmul(stacked(q_ref, unit), k_all[places(unit)[1]], NT)

        def softmax(unit, s):
            _, keys, _ = places(unit)
            width = keys.stop - keys.start
            shut = bias[unit[0], :, keys.start - unit[0] * TILE :]
            s = s.reshape(per_call, TILE, width) * FACTOR2 + shut[None]
            s = s.reshape(per_call * TILE, width)
            e = jnp.exp2(s - jnp.max(s, 1, keepdims=True))
            return e * (1.0 / jnp.sum(e, 1, keepdims=True))

        def score_grads(unit, weight):
            here, keys, cols = places(unit)
            do = stacked(do_ref, unit)
            out = matmul(weight, v_all[keys], NN).astype(jnp.bfloat16)
            for x, c in enumerate(cols):
                o_ref[group, here, c] = out[x * TILE : (x + 1) * TILE]
            dp = matmul(do, v_all[keys], NT)
            delta = jnp.sum(out.astype(jnp.float32) * do.astype(jnp.float32), 1, keepdims=True)
            ds = weight * (dp - delta).astype(jnp.bfloat16)
            tile, first = unit
            ds_ref[group, tile, first * TILE : (first + per_call) * TILE, keys.start - tile * TILE :] = ds
            return ds

        def sums(unit, weight, ds):
            _, keys, _ = places(unit)
            dv_sum[:, keys] += matmul(stacked(do_ref, unit), weight, TN)
            dk_sum[:, keys] += matmul(stacked(q_ref, unit), ds, TN)

        ahead = scores(units[0])
        before = None
        for index, unit in enumerate(units):
            now = ahead
            if index + 1 < len(units):
                ahead = scores(units[index + 1])
            weight = softmax(unit, now).astype(jnp.bfloat16)
            if before is not None:
                sums(*before)
            before = (unit, weight, score_grads(unit, weight))
        sums(*before)
        if lowest:
            for tile in range(tiles):
                gap = max(0, lowest - tile * TILE)
                ds_ref[group, tile, :, :gap] = jnp.zeros((heads * TILE, gap), jnp.bfloat16)

        here = lanes(group)
        own_ref[0, :, here] = dk_sum[:, 2 * rows :].T * FACTOR
        own_ref[1, :, here] = dv_sum[:, 2 * rows :].T
        for place in range(2):
            span = slice(place * rows, (place + 1) * rows)
            back_ref[place, 0, :, here] = (dk_sum[:, span].T * FACTOR).astype(jnp.bfloat16)
            back_ref[place, 1, :, here] = dv_sum[:, span].T.astype(jnp.bfloat16)

    @pl.when(first_ref[0] >= 2 * rows)
    def _():
        all_units(0)

    @pl.when(first_ref[0] < 2 * rows)
    def _():
        all_units(rows)

    @pl.when(group == groups - 1)
    def _():
        for fetch in fetches:
            fetch.wait()


def attention(base, groups, skipped, head_cols, first, bias, q, do, far, near, own, whole_q=None, whole_do=None):
    rows = q.shape[0]
    tiles, _, band = bias.shape
    whole = pl.BlockSpec(memory_space=pltpu.VMEM)
    fetching = whole_q is not None
    far_away = pl.BlockSpec(memory_space=pltpu.HBM)
    rest = (rows, whole_q.shape[1] - q.shape[1] if fetching else 0)
    return pl.pallas_call(
        functools.partial(attention_kernel, base, skipped, fetching),
        grid=(groups,),
        in_specs=[pl.BlockSpec(memory_space=pltpu.SMEM), whole, whole, whole, whole, whole, whole] + [far_away, far_away] * fetching,
        out_specs=[whole] * (6 if fetching else 4),
        out_shape=[
            jax.ShapeDtypeStruct((groups, rows, head_cols), jnp.bfloat16),
            jax.ShapeDtypeStruct((groups, tiles, head_cols // HEAD_DIM * TILE, band), jnp.bfloat16),
            jax.ShapeDtypeStruct((2, 2, rows, groups * HEAD_DIM), jnp.bfloat16),
            jax.ShapeDtypeStruct((2, rows, groups * HEAD_DIM), jnp.float32),
        ]
        + [jax.ShapeDtypeStruct(rest, q.dtype)] * (2 if fetching else 0),
        scratch_shapes=[
            pltpu.VMEM((3 * rows, HEAD_DIM), jnp.bfloat16),
            pltpu.VMEM((3 * rows, HEAD_DIM), jnp.bfloat16),
            pltpu.VMEM((HEAD_DIM, 3 * rows), jnp.float32),
            pltpu.VMEM((HEAD_DIM, 3 * rows), jnp.float32),
        ]
        + [pltpu.SemaphoreType.DMA((2,))] * fetching,
        compiler_params=pltpu.CompilerParams(vmem_limit_bytes=VMEM_LIMIT),
        name="attention",
    )(first, bias, q, do, far, near, own, *((whole_q, whole_do) if fetching else ()))


def query_kernel(calls, skips, *refs):
    o_out, dq_out, k_all, held, sems = refs[-5:]
    rows = held.shape[0]
    wide = held.shape[1] // sum(calls)
    groups = [(index, here) for index, size in enumerate(calls) for here in range(size)]
    copies = []
    for place, (index, here) in enumerate(groups):
        cols = pl.ds(place * wide, wide)
        copies.append(pltpu.make_async_copy(refs[5 * index].at[here], o_out.at[:, cols], sems.at[place, 0]))
        copies[-1].start()
    for place, (index, here) in enumerate(groups):
        _, ds_ref, *parts = refs[5 * index : 5 * index + 5]
        column = slice((skips[index] + here) * HEAD_DIM, (skips[index] + here + 1) * HEAD_DIM)
        for spot, part in enumerate(parts):
            k_all[spot * rows : (spot + 1) * rows] = part[:, column]
        for tile in range(ds_ref.shape[1]):
            k = k_all[tile * TILE : tile * TILE + ds_ref.shape[3]]
            dq = (matmul(ds_ref[here, tile], k, NN) * FACTOR).astype(jnp.bfloat16)
            for x in range(wide // HEAD_DIM):
                start = place * wide + x * HEAD_DIM
                held[tile * TILE : (tile + 1) * TILE, start : start + HEAD_DIM] = dq[x * TILE : (x + 1) * TILE]
        cols = pl.ds(place * wide, wide)
        copies.append(pltpu.make_async_copy(held.at[:, cols], dq_out.at[:, cols], sems.at[place, 1]))
        copies[-1].start()
    for copy in copies:
        copy.wait()


def query_grads(calls, skips, shape, parts):
    rows, width = shape
    flat = [array for part in parts for array in part]
    return pl.pallas_call(
        functools.partial(query_kernel, calls, skips),
        in_specs=[pl.BlockSpec(memory_space=pltpu.VMEM)] * len(flat),
        out_specs=[pl.BlockSpec(memory_space=pltpu.HBM)] * 2,
        out_shape=[jax.ShapeDtypeStruct(shape, jnp.bfloat16)] * 2,
        scratch_shapes=[
            pltpu.VMEM((3 * rows, HEAD_DIM), jnp.bfloat16),
            pltpu.VMEM(shape, jnp.bfloat16),
            pltpu.SemaphoreType.DMA((sum(calls), 2)),
        ],
        compiler_params=pltpu.CompilerParams(vmem_limit_bytes=QUERY_LIMIT),
        name="query_grads",
    )(*flat)


def finish_kernel(base, aliased, *refs):
    refs = refs[2:] if aliased else refs
    kept_ref, returned_ref, gk_ref, gv_ref, total, sems = refs
    span = pl.ds(base * HEAD_DIM, kept_ref.shape[2])
    copies = []
    for index, out in enumerate((gk_ref, gv_ref)):
        total[index] = (kept_ref[index] + returned_ref[index].astype(jnp.float32)).astype(jnp.bfloat16)
        copies.append(pltpu.make_async_copy(total.at[index], out.at[:, span], sems.at[index]))
        copies[-1].start()
    for copy in copies:
        copy.wait()


def finished(base, shape, kept, returned, carried):
    aliased = carried is not None
    carried = carried if aliased else ()
    kept_place = pl.BlockSpec(memory_space=pl.ANY)
    whole = pl.BlockSpec(memory_space=pltpu.VMEM)
    return pl.pallas_call(
        functools.partial(finish_kernel, base, aliased),
        in_specs=[kept_place] * len(carried) + [whole, whole],
        out_specs=[pl.BlockSpec(memory_space=pltpu.HBM)] * 2,
        out_shape=[jax.ShapeDtypeStruct(shape, jnp.bfloat16)] * 2,
        scratch_shapes=[
            pltpu.VMEM((2, shape[0], kept.shape[2]), jnp.bfloat16),
            pltpu.SemaphoreType.DMA((2,)),
        ],
        input_output_aliases={0: 0, 1: 1} if aliased else {},
        compiler_params=pltpu.CompilerParams(vmem_limit_bytes=SMALL_LIMIT),
        name="finish_keys_values",
    )(*carried, kept, returned)


def on_device(queries, keys, values, grad_out, episode_lengths):
    rows = queries.shape[0]
    groups = keys.shape[1] // HEAD_DIM
    count = lax.axis_size("seq")
    place = lax.axis_index("seq").astype(jnp.int32)
    odd = lax.bitwise_and(place, jnp.int32(1))
    first = jnp.reshape(place * rows, (1,))
    ahead = [(source, (source + 2) % count) for source in range(count)]
    behind = [((source + 2) % count, source) for source in range(count)]
    ahead_open = ahead[: count - 2]
    behind_open = behind[: count - 2]
    swap = [(source, source ^ 1) for source in range(count)]
    known = groups == sum(SENT)
    sent = SENT if known else (groups,)
    calls = CALLS if known else (groups,)
    returns = RETURNED if known else (groups,)
    starts = [sum(sent[:index]) for index in range(len(sent))]

    q_here, do_here, k_here, v_here = (in_hbm(x) for x in (queries, grad_out, keys, values))
    own = list(packed(k_here, v_here, [start * HEAD_DIM for start in starts], [size * HEAD_DIM for size in sent]))
    far = [permuted(block, ahead_open if index else ahead) for index, block in enumerate(own)]
    head_cols = queries.shape[1] // groups
    bias, q_part, do_part = prepared(episode_lengths, first, q_here, do_here, calls[0] * head_cols)
    own[0], bias = lax.optimization_barrier((own[0], bias))
    near = []
    grads = None
    parts = []
    waiting = []
    stored = []
    skips = []
    base = begun = 0
    for size in calls:
        chunk = max(index for index, start in enumerate(starts) if start <= base)
        skips.append(base - starts[chunk])
        if chunk == len(near):
            there = far[chunk]
            if stored:
                there, ds = lax.optimization_barrier((there, stored[-1][1]))
                stored[-1] = (stored[-1][0], ds) + stored[-1][2:]
            near.append(permuted(jnp.where(odd == 1, there, own[chunk]), swap))
        if base == 0 and size < groups:
            out, ds, back, kept, q_part, do_part = attention(
                0, size, skips[-1], head_cols, first, bias, q_part, do_part, far[chunk], near[chunk], own[chunk], q_here, do_here
            )
        else:
            out, ds, back, kept = attention(
                base - (calls[0] if base else 0), size, skips[-1], head_cols, first, bias, q_part, do_part, far[chunk], near[chunk], own[chunk]
            )
        stored.append((out, ds, far[chunk], near[chunk], own[chunk]))
        waiting.append((back, kept))
        base += size
        if base < begun + returns[len(parts)]:
            continue
        back = jnp.concatenate([pair[0] for pair in waiting], axis=3)
        kept = jnp.concatenate([pair[1] for pair in waiting], axis=2)
        waiting = []
        if parts:
            back, parts[-1][2] = lax.optimization_barrier((back, parts[-1][2]))
        beside = permuted(back[1], swap)
        none = jnp.zeros_like(beside)
        onward = back[0].astype(jnp.float32) + jnp.where(odd == 1, beside, none).astype(jnp.float32)
        kept = kept + jnp.where(odd == 1, none, beside).astype(jnp.float32)
        parts.append([begun, kept, permuted(onward.astype(jnp.bfloat16), behind_open if parts else behind)])
        begun = base
    attn_out, grad_queries = query_grads(calls, skips, queries.shape, stored)
    for begun, kept, returned in parts:
        grads = finished(begun, keys.shape, kept, returned, grads)
    return (attn_out, grad_queries, *grads)


def solution(mesh):
    split = P(("groups", "seq"), None)
    return jax.shard_map(
        on_device,
        mesh=mesh,
        in_specs=(split, split, split, split, P("groups")),
        out_specs=(split, split, split, split),
        check_vma=False,
    )
```

```python
import functools
import math

import jax
import jax.numpy as jnp
from jax import lax
from jax.experimental import pallas as pl
from jax.experimental.pallas import tpu as pltpu
from jax.sharding import PartitionSpec as P

HEAD_DIM = 128
TILE = 128
HEADS_AT_ONCE = 4
SENT = (1, 3)
CALLS = (1, 3)
RETURNED = (1, 3)
NT = (((1,), (1,)), ((), ()))
NN = (((1,), (0,)), ((), ()))
TN = (((0,), (0,)), ((), ()))
FACTOR = 1.0 / math.sqrt(HEAD_DIM)
FACTOR2 = math.log2(math.e) / math.sqrt(HEAD_DIM)
NEVER = -1e30
VMEM_LIMIT = 20 * 1024 * 1024
QUERY_LIMIT = 12 * 1024 * 1024
SMALL_LIMIT = 8 * 1024 * 1024


def matmul(left, right, dims):
    return lax.dot_general(left, right, dims, preferred_element_type=jnp.float32)


def permuted(value, pairs):
    return lax.ppermute(value, "seq", pairs)


def in_hbm(value):
    return pltpu.with_memory_space_constraint(value, pltpu.HBM)


def pack_kernel(starts, sizes, k_hbm, v_hbm, *refs):
    outs, sems = refs[:-1], refs[-1]
    copies = []
    for index, (start, size) in enumerate(zip(starts, sizes)):
        for place, whole in enumerate((k_hbm, v_hbm)):
            held = outs[index].at[:, pl.ds(place * size, size)]
            copies.append(pltpu.make_async_copy(whole.at[:, pl.ds(start, size)], held, sems.at[index, place]))
            copies[-1].start()
    for copy in copies:
        copy.wait()


def packed(keys, values, starts, sizes):
    rows = keys.shape[0]
    return pl.pallas_call(
        functools.partial(pack_kernel, starts, sizes),
        in_specs=[pl.BlockSpec(memory_space=pltpu.HBM)] * 2,
        out_specs=[pl.BlockSpec(memory_space=pltpu.VMEM)] * len(sizes),
        out_shape=[jax.ShapeDtypeStruct((rows, 2 * size), keys.dtype) for size in sizes],
        scratch_shapes=[pltpu.SemaphoreType.DMA((len(sizes), 2))],
        compiler_params=pltpu.CompilerParams(vmem_limit_bytes=SMALL_LIMIT),
        name="pack_keys_values",
    )(keys, values)


def prepare_kernel(count, lengths_ref, first_ref, q_hbm, do_hbm, bias_ref, q_ref, do_ref, sems):
    span = pl.ds(0, q_ref.shape[1])
    fetches = [
        pltpu.make_async_copy(whole.at[:, span], held, sems.at[index])
        for index, (whole, held) in enumerate(((q_hbm, q_ref), (do_hbm, do_ref)))
    ]
    for fetch in fetches:
        fetch.start()
    tiles, _, band = bias_ref.shape
    rows = tiles * TILE
    row = lax.broadcasted_iota(jnp.int32, (rows, 1), 0)

    def one(index, carry):
        begin, start = carry
        return begin + lengths_ref[index], jnp.where(row >= begin, begin, start)

    _, start = lax.fori_loop(
        0, count, one, (-first_ref[0], jnp.full((rows, 1), -4 * rows, jnp.int32))
    )
    for tile in range(tiles):
        here = slice(tile * TILE, (tile + 1) * TILE)
        key = lax.broadcasted_iota(jnp.int32, (TILE, band), 1) + (tile * TILE - 2 * rows)
        allowed = (key >= start[here]) & (key <= row[here])
        bias_ref[tile] = jnp.where(allowed, 0.0, NEVER)
    for fetch in fetches:
        fetch.wait()


def prepared(lengths, first, q, do, width):
    rows = q.shape[0]
    smem = pl.BlockSpec(memory_space=pltpu.SMEM)
    far_away = pl.BlockSpec(memory_space=pltpu.HBM)
    whole = pl.BlockSpec(memory_space=pltpu.VMEM)
    return pl.pallas_call(
        functools.partial(prepare_kernel, lengths.shape[0]),
        in_specs=[smem, smem, far_away, far_away],
        out_specs=[whole] * 3,
        out_shape=[
            jax.ShapeDtypeStruct((rows // TILE, TILE, 2 * rows + TILE), jnp.float32),
            jax.ShapeDtypeStruct((rows, width), q.dtype),
            jax.ShapeDtypeStruct((rows, width), do.dtype),
        ],
        scratch_shapes=[pltpu.SemaphoreType.DMA((2,))],
        compiler_params=pltpu.CompilerParams(vmem_limit_bytes=SMALL_LIMIT),
        name="prepare",
    )(lengths, first, q, do)


def lanes(block, width=HEAD_DIM):
    return pl.ds(pl.multiple_of(block * width, width), width)


def attention_kernel(base, skipped, fetching, first_ref, bias, q_ref, do_ref, far, near, own, *refs):
    fetches = []
    if fetching:
        q_hbm, do_hbm, *refs, sems = refs
        q_rest, do_rest = refs[4:6]
        refs = refs[:4] + refs[6:]
        span = pl.ds(q_ref.shape[1], q_rest.shape[1])
        for index, (whole, held) in enumerate(((q_hbm, q_rest), (do_hbm, do_rest))):
            fetches.append(pltpu.make_async_copy(whole.at[:, span], held, sems.at[index]))
    o_ref, ds_ref, back_ref, own_ref, k_all, v_all, dk_sum, dv_sum = refs
    group = pl.program_id(0)
    groups, tiles, _, _ = ds_ref.shape
    rows = far.shape[0]
    sent = far.shape[1] // (2 * HEAD_DIM)
    wide = o_ref.shape[2]
    heads = wide // HEAD_DIM
    per_call = min(HEADS_AT_ONCE, heads)
    @pl.when(group == 0)
    def _():
        for fetch in fetches:
            fetch.start()

    k_col = lanes(skipped + group)
    v_col = lanes(sent + skipped + group)
    for place, part in enumerate((far, near, own)):
        k_all[place * rows : (place + 1) * rows] = part[:, k_col]
        v_all[place * rows : (place + 1) * rows] = part[:, v_col]

    def all_units(lowest):
        dk_sum[...] = jnp.zeros_like(dk_sum)
        dv_sum[...] = jnp.zeros_like(dv_sum)
        units = [(tile, first) for tile in range(tiles) for first in range(0, heads, per_call)]

        def places(unit):
            tile, first = unit
            here = slice(tile * TILE, (tile + 1) * TILE)
            keys = slice(max(tile * TILE, lowest), tile * TILE + 2 * rows + TILE)
            cols = [slice((first + x) * HEAD_DIM, (first + x + 1) * HEAD_DIM) for x in range(per_call)]
            return here, keys, cols

        def stacked(ref, unit):
            here, _, cols = places(unit)
            first = (base + group) * heads
            return jnp.concatenate([ref[here, lanes(first + c.start // HEAD_DIM)] for c in cols], 0)

        def scores(unit):
            return matmul(stacked(q_ref, unit), k_all[places(unit)[1]], NT)

        def softmax(unit, s):
            _, keys, _ = places(unit)
            width = keys.stop - keys.start
            shut = bias[unit[0], :, keys.start - unit[0] * TILE :]
            s = s.reshape(per_call, TILE, width) * FACTOR2 + shut[None]
            s = s.reshape(per_call * TILE, width)
            e = jnp.exp2(s - jnp.max(s, 1, keepdims=True))
            return e * (1.0 / jnp.sum(e, 1, keepdims=True))

        def score_grads(unit, weight):
            here, keys, cols = places(unit)
            do = stacked(do_ref, unit)
            out = matmul(weight, v_all[keys], NN).astype(jnp.bfloat16)
            for x, c in enumerate(cols):
                o_ref[group, here, c] = out[x * TILE : (x + 1) * TILE]
            dp = matmul(do, v_all[keys], NT)
            delta = jnp.sum(out.astype(jnp.float32) * do.astype(jnp.float32), 1, keepdims=True)
            ds = weight * (dp - delta).astype(jnp.bfloat16)
            tile, first = unit
            ds_ref[group, tile, first * TILE : (first + per_call) * TILE, keys.start - tile * TILE :] = ds
            return ds

        def sums(unit, weight, ds):
            _, keys, _ = places(unit)
            dv_sum[:, keys] += matmul(stacked(do_ref, unit), weight, TN)
            dk_sum[:, keys] += matmul(stacked(q_ref, unit), ds, TN)

        last = len(units) - 1
        weight = softmax(units[0], scores(units[0])).astype(jnp.bfloat16)
        ahead = scores(units[1]) if last else None
        before = None
        for index, unit in enumerate(units):
            if index < last:
                following = softmax(units[index + 1], ahead).astype(jnp.bfloat16)
            if index + 1 < last:
                ahead = scores(units[index + 2])
            if before is not None:
                sums(*before)
            before = (unit, weight, score_grads(unit, weight))
            weight = following if index < last else None
        sums(*before)
        if lowest:
            for tile in range(tiles):
                gap = max(0, lowest - tile * TILE)
                ds_ref[group, tile, :, :gap] = jnp.zeros((heads * TILE, gap), jnp.bfloat16)

        here = lanes(group)
        own_ref[0, :, here] = dk_sum[:, 2 * rows :].T * FACTOR
        own_ref[1, :, here] = dv_sum[:, 2 * rows :].T
        for place in range(2):
            span = slice(place * rows, (place + 1) * rows)
            back_ref[place, 0, :, here] = (dk_sum[:, span].T * FACTOR).astype(jnp.bfloat16)
            back_ref[place, 1, :, here] = dv_sum[:, span].T.astype(jnp.bfloat16)

    @pl.when(first_ref[0] >= 2 * rows)
    def _():
        all_units(0)

    @pl.when(first_ref[0] < 2 * rows)
    def _():
        all_units(rows)

    @pl.when(group == groups - 1)
    def _():
        for fetch in fetches:
            fetch.wait()


def attention(base, groups, skipped, head_cols, first, bias, q, do, far, near, own, whole_q=None, whole_do=None):
    rows = q.shape[0]
    tiles, _, band = bias.shape
    whole = pl.BlockSpec(memory_space=pltpu.VMEM)
    fetching = whole_q is not None
    far_away = pl.BlockSpec(memory_space=pltpu.HBM)
    rest = (rows, whole_q.shape[1] - q.shape[1] if fetching else 0)
    return pl.pallas_call(
        functools.partial(attention_kernel, base, skipped, fetching),
        grid=(groups,),
        in_specs=[pl.BlockSpec(memory_space=pltpu.SMEM), whole, whole, whole, whole, whole, whole] + [far_away, far_away] * fetching,
        out_specs=[whole] * (6 if fetching else 4),
        out_shape=[
            jax.ShapeDtypeStruct((groups, rows, head_cols), jnp.bfloat16),
            jax.ShapeDtypeStruct((groups, tiles, head_cols // HEAD_DIM * TILE, band), jnp.bfloat16),
            jax.ShapeDtypeStruct((2, 2, rows, groups * HEAD_DIM), jnp.bfloat16),
            jax.ShapeDtypeStruct((2, rows, groups * HEAD_DIM), jnp.float32),
        ]
        + [jax.ShapeDtypeStruct(rest, q.dtype)] * (2 if fetching else 0),
        scratch_shapes=[
            pltpu.VMEM((3 * rows, HEAD_DIM), jnp.bfloat16),
            pltpu.VMEM((3 * rows, HEAD_DIM), jnp.bfloat16),
            pltpu.VMEM((HEAD_DIM, 3 * rows), jnp.float32),
            pltpu.VMEM((HEAD_DIM, 3 * rows), jnp.float32),
        ]
        + [pltpu.SemaphoreType.DMA((2,))] * fetching,
        compiler_params=pltpu.CompilerParams(vmem_limit_bytes=VMEM_LIMIT),
        name="attention",
    )(first, bias, q, do, far, near, own, *((whole_q, whole_do) if fetching else ()))


def query_kernel(calls, skips, *refs):
    o_out, dq_out, k_all, held, sems = refs[-5:]
    rows = held.shape[0]
    wide = held.shape[1] // sum(calls)
    groups = [(index, here) for index, size in enumerate(calls) for here in range(size)]
    copies = []
    for place, (index, here) in enumerate(groups):
        cols = pl.ds(place * wide, wide)
        copies.append(pltpu.make_async_copy(refs[5 * index].at[here], o_out.at[:, cols], sems.at[place, 0]))
        copies[-1].start()
    for place, (index, here) in enumerate(groups):
        _, ds_ref, *parts = refs[5 * index : 5 * index + 5]
        column = slice((skips[index] + here) * HEAD_DIM, (skips[index] + here + 1) * HEAD_DIM)
        for spot, part in enumerate(parts):
            k_all[spot * rows : (spot + 1) * rows] = part[:, column]
        for tile in range(ds_ref.shape[1]):
            k = k_all[tile * TILE : tile * TILE + ds_ref.shape[3]]
            dq = (matmul(ds_ref[here, tile], k, NN) * FACTOR).astype(jnp.bfloat16)
            for x in range(wide // HEAD_DIM):
                start = place * wide + x * HEAD_DIM
                held[tile * TILE : (tile + 1) * TILE, start : start + HEAD_DIM] = dq[x * TILE : (x + 1) * TILE]
        cols = pl.ds(place * wide, wide)
        copies.append(pltpu.make_async_copy(held.at[:, cols], dq_out.at[:, cols], sems.at[place, 1]))
        copies[-1].start()
    for copy in copies:
        copy.wait()


def query_grads(calls, skips, shape, parts):
    rows, width = shape
    flat = [array for part in parts for array in part]
    return pl.pallas_call(
        functools.partial(query_kernel, calls, skips),
        in_specs=[pl.BlockSpec(memory_space=pltpu.VMEM)] * len(flat),
        out_specs=[pl.BlockSpec(memory_space=pltpu.HBM)] * 2,
        out_shape=[jax.ShapeDtypeStruct(shape, jnp.bfloat16)] * 2,
        scratch_shapes=[
            pltpu.VMEM((3 * rows, HEAD_DIM), jnp.bfloat16),
            pltpu.VMEM(shape, jnp.bfloat16),
            pltpu.SemaphoreType.DMA((sum(calls), 2)),
        ],
        compiler_params=pltpu.CompilerParams(vmem_limit_bytes=QUERY_LIMIT),
        name="query_grads",
    )(*flat)


def finish_kernel(base, aliased, *refs):
    refs = refs[2:] if aliased else refs
    kept_ref, returned_ref, gk_ref, gv_ref, total, sems = refs
    span = pl.ds(base * HEAD_DIM, kept_ref.shape[2])
    copies = []
    for index, out in enumerate((gk_ref, gv_ref)):
        total[index] = (kept_ref[index] + returned_ref[index].astype(jnp.float32)).astype(jnp.bfloat16)
        copies.append(pltpu.make_async_copy(total.at[index], out.at[:, span], sems.at[index]))
        copies[-1].start()
    for copy in copies:
        copy.wait()


def finished(base, shape, kept, returned, carried):
    aliased = carried is not None
    carried = carried if aliased else ()
    kept_place = pl.BlockSpec(memory_space=pl.ANY)
    whole = pl.BlockSpec(memory_space=pltpu.VMEM)
    return pl.pallas_call(
        functools.partial(finish_kernel, base, aliased),
        in_specs=[kept_place] * len(carried) + [whole, whole],
        out_specs=[pl.BlockSpec(memory_space=pltpu.HBM)] * 2,
        out_shape=[jax.ShapeDtypeStruct(shape, jnp.bfloat16)] * 2,
        scratch_shapes=[
            pltpu.VMEM((2, shape[0], kept.shape[2]), jnp.bfloat16),
            pltpu.SemaphoreType.DMA((2,)),
        ],
        input_output_aliases={0: 0, 1: 1} if aliased else {},
        compiler_params=pltpu.CompilerParams(vmem_limit_bytes=SMALL_LIMIT),
        name="finish_keys_values",
    )(*carried, kept, returned)


def on_device(queries, keys, values, grad_out, episode_lengths):
    rows = queries.shape[0]
    groups = keys.shape[1] // HEAD_DIM
    count = lax.axis_size("seq")
    place = lax.axis_index("seq").astype(jnp.int32)
    odd = lax.bitwise_and(place, jnp.int32(1))
    first = jnp.reshape(place * rows, (1,))
    ahead = [(source, (source + 2) % count) for source in range(count)]
    behind = [((source + 2) % count, source) for source in range(count)]
    ahead_open = ahead[: count - 2]
    behind_open = behind[: count - 2]
    swap = [(source, source ^ 1) for source in range(count)]
    known = groups == sum(SENT)
    sent = SENT if known else (groups,)
    calls = CALLS if known else (groups,)
    returns = RETURNED if known else (groups,)
    starts = [sum(sent[:index]) for index in range(len(sent))]

    q_here, do_here, k_here, v_here = (in_hbm(x) for x in (queries, grad_out, keys, values))
    own = list(packed(k_here, v_here, [start * HEAD_DIM for start in starts], [size * HEAD_DIM for size in sent]))
    far = [permuted(block, ahead_open if index else ahead) for index, block in enumerate(own)]
    head_cols = queries.shape[1] // groups
    bias, q_part, do_part = prepared(episode_lengths, first, q_here, do_here, calls[0] * head_cols)
    own[0], bias = lax.optimization_barrier((own[0], bias))
    near = []
    grads = None
    parts = []
    waiting = []
    stored = []
    skips = []
    base = begun = 0
    for size in calls:
        chunk = max(index for index, start in enumerate(starts) if start <= base)
        skips.append(base - starts[chunk])
        if chunk == len(near):
            there = far[chunk]
            if stored:
                there, ds = lax.optimization_barrier((there, stored[-1][1]))
                stored[-1] = (stored[-1][0], ds) + stored[-1][2:]
            near.append(permuted(jnp.where(odd == 1, there, own[chunk]), swap))
        if base == 0 and size < groups:
            out, ds, back, kept, q_part, do_part = attention(
                0, size, skips[-1], head_cols, first, bias, q_part, do_part, far[chunk], near[chunk], own[chunk], q_here, do_here
            )
        else:
            out, ds, back, kept = attention(
                base - (calls[0] if base else 0), size, skips[-1], head_cols, first, bias, q_part, do_part, far[chunk], near[chunk], own[chunk]
            )
        stored.append((out, ds, far[chunk], near[chunk], own[chunk]))
        waiting.append((back, kept))
        base += size
        if base < begun + returns[len(parts)]:
            continue
        back = jnp.concatenate([pair[0] for pair in waiting], axis=3)
        kept = jnp.concatenate([pair[1] for pair in waiting], axis=2)
        waiting = []
        if parts:
            back, parts[-1][2] = lax.optimization_barrier((back, parts[-1][2]))
        beside = permuted(back[1], swap)
        none = jnp.zeros_like(beside)
        onward = back[0].astype(jnp.float32) + jnp.where(odd == 1, beside, none).astype(jnp.float32)
        kept = kept + jnp.where(odd == 1, none, beside).astype(jnp.float32)
        parts.append([begun, kept, permuted(onward.astype(jnp.bfloat16), behind_open if parts else behind)])
        begun = base
    attn_out, grad_queries = query_grads(calls, skips, queries.shape, stored)
    for begun, kept, returned in parts:
        grads = finished(begun, keys.shape, kept, returned, grads)
    return (attn_out, grad_queries, *grads)


def solution(mesh):
    split = P(("groups", "seq"), None)
    return jax.shard_map(
        on_device,
        mesh=mesh,
        in_specs=(split, split, split, split, P("groups")),
        out_specs=(split, split, split, split),
        check_vma=False,
    )
```

```python
import functools
import math

import jax
import jax.numpy as jnp
from jax import lax
from jax.experimental import pallas as pl
from jax.experimental.pallas import tpu as pltpu
from jax.sharding import PartitionSpec as P

HEAD_DIM = 128
TILE = 128
HEADS_AT_ONCE = 4
SENT = (1, 3)
CALLS = (1, 3)
RETURNED = (1, 3)
NT = (((1,), (1,)), ((), ()))
NN = (((1,), (0,)), ((), ()))
TN = (((0,), (0,)), ((), ()))
FACTOR = 1.0 / math.sqrt(HEAD_DIM)
FACTOR2 = math.log2(math.e) / math.sqrt(HEAD_DIM)
NEVER = -1e30
VMEM_LIMIT = 20 * 1024 * 1024
QUERY_LIMIT = 12 * 1024 * 1024
SMALL_LIMIT = 8 * 1024 * 1024


def matmul(left, right, dims):
    return lax.dot_general(left, right, dims, preferred_element_type=jnp.float32)


def permuted(value, pairs):
    return lax.ppermute(value, "seq", pairs)


def in_hbm(value):
    return pltpu.with_memory_space_constraint(value, pltpu.HBM)


def pack_kernel(starts, sizes, k_hbm, v_hbm, *refs):
    outs, sems = refs[:-1], refs[-1]
    copies = []
    for index, (start, size) in enumerate(zip(starts, sizes)):
        for place, whole in enumerate((k_hbm, v_hbm)):
            held = outs[index].at[:, pl.ds(place * size, size)]
            copies.append(pltpu.make_async_copy(whole.at[:, pl.ds(start, size)], held, sems.at[index, place]))
            copies[-1].start()
    for copy in copies:
        copy.wait()


def packed(keys, values, starts, sizes):
    rows = keys.shape[0]
    return pl.pallas_call(
        functools.partial(pack_kernel, starts, sizes),
        in_specs=[pl.BlockSpec(memory_space=pltpu.HBM)] * 2,
        out_specs=[pl.BlockSpec(memory_space=pltpu.VMEM)] * len(sizes),
        out_shape=[jax.ShapeDtypeStruct((rows, 2 * size), keys.dtype) for size in sizes],
        scratch_shapes=[pltpu.SemaphoreType.DMA((len(sizes), 2))],
        compiler_params=pltpu.CompilerParams(vmem_limit_bytes=SMALL_LIMIT),
        name="pack_keys_values",
    )(keys, values)


def prepare_kernel(count, lengths_ref, first_ref, q_hbm, do_hbm, bias_ref, q_ref, do_ref, sems):
    span = pl.ds(0, q_ref.shape[1])
    fetches = [
        pltpu.make_async_copy(whole.at[:, span], held, sems.at[index])
        for index, (whole, held) in enumerate(((q_hbm, q_ref), (do_hbm, do_ref)))
    ]
    for fetch in fetches:
        fetch.start()
    tiles, _, band = bias_ref.shape
    rows = tiles * TILE
    row = lax.broadcasted_iota(jnp.int32, (rows, 1), 0)

    def one(index, carry):
        begin, start = carry
        return begin + lengths_ref[index], jnp.where(row >= begin, begin, start)

    _, start = lax.fori_loop(
        0, count, one, (-first_ref[0], jnp.full((rows, 1), -4 * rows, jnp.int32))
    )
    for tile in range(tiles):
        here = slice(tile * TILE, (tile + 1) * TILE)
        key = lax.broadcasted_iota(jnp.int32, (TILE, band), 1) + (tile * TILE - 2 * rows)
        allowed = (key >= start[here]) & (key <= row[here])
        bias_ref[tile] = jnp.where(allowed, 0.0, NEVER)
    for fetch in fetches:
        fetch.wait()


def prepared(lengths, first, q, do, width):
    rows = q.shape[0]
    smem = pl.BlockSpec(memory_space=pltpu.SMEM)
    far_away = pl.BlockSpec(memory_space=pltpu.HBM)
    whole = pl.BlockSpec(memory_space=pltpu.VMEM)
    return pl.pallas_call(
        functools.partial(prepare_kernel, lengths.shape[0]),
        in_specs=[smem, smem, far_away, far_away],
        out_specs=[whole] * 3,
        out_shape=[
            jax.ShapeDtypeStruct((rows // TILE, TILE, 2 * rows + TILE), jnp.float32),
            jax.ShapeDtypeStruct((rows, width), q.dtype),
            jax.ShapeDtypeStruct((rows, width), do.dtype),
        ],
        scratch_shapes=[pltpu.SemaphoreType.DMA((2,))],
        compiler_params=pltpu.CompilerParams(vmem_limit_bytes=SMALL_LIMIT),
        name="prepare",
    )(lengths, first, q, do)


def lanes(block, width=HEAD_DIM):
    return pl.ds(pl.multiple_of(block * width, width), width)


def attention_kernel(base, skipped, fetching, first_ref, bias, q_ref, do_ref, far, near, own, *refs):
    fetches = []
    if fetching:
        q_hbm, do_hbm, *refs, sems = refs
        q_rest, do_rest = refs[4:6]
        refs = refs[:4] + refs[6:]
        span = pl.ds(q_ref.shape[1], q_rest.shape[1])
        for index, (whole, held) in enumerate(((q_hbm, q_rest), (do_hbm, do_rest))):
            fetches.append(pltpu.make_async_copy(whole.at[:, span], held, sems.at[index]))
    o_ref, ds_ref, back_ref, own_ref, k_all, v_all, dk_sum, dv_sum = refs
    group = pl.program_id(0)
    groups, tiles, _, _ = ds_ref.shape
    rows = far.shape[0]
    sent = far.shape[1] // (2 * HEAD_DIM)
    wide = o_ref.shape[2]
    heads = wide // HEAD_DIM
    per_call = min(HEADS_AT_ONCE, heads)
    @pl.when(group == 0)
    def _():
        for fetch in fetches:
            fetch.start()

    k_col = lanes(skipped + group)
    v_col = lanes(sent + skipped + group)
    for place, part in enumerate((far, near, own)):
        k_all[place * rows : (place + 1) * rows] = part[:, k_col]
        v_all[place * rows : (place + 1) * rows] = part[:, v_col]

    def all_units(lowest):
        dk_sum[...] = jnp.zeros_like(dk_sum)
        dv_sum[...] = jnp.zeros_like(dv_sum)
        units = [(tile, first) for tile in range(tiles) for first in range(0, heads, per_call)]

        def places(unit):
            tile, first = unit
            here = slice(tile * TILE, (tile + 1) * TILE)
            keys = slice(max(tile * TILE, lowest), tile * TILE + 2 * rows + TILE)
            cols = [slice((first + x) * HEAD_DIM, (first + x + 1) * HEAD_DIM) for x in range(per_call)]
            return here, keys, cols

        def stacked(ref, unit):
            here, _, cols = places(unit)
            first = (base + group) * heads
            return jnp.concatenate([ref[here, lanes(first + c.start // HEAD_DIM)] for c in cols], 0)

        def scores(unit):
            return matmul(stacked(q_ref, unit), k_all[places(unit)[1]], NT)

        def softmax(unit, s):
            _, keys, _ = places(unit)
            width = keys.stop - keys.start
            shut = bias[unit[0], :, keys.start - unit[0] * TILE :]
            s = s.reshape(per_call, TILE, width) * FACTOR2 + shut[None]
            s = s.reshape(per_call * TILE, width)
            e = jnp.exp2(s - jnp.max(s, 1, keepdims=True))
            return e * (1.0 / jnp.sum(e, 1, keepdims=True))

        def score_grads(unit, weight):
            here, keys, cols = places(unit)
            do = stacked(do_ref, unit)
            out = matmul(weight, v_all[keys], NN).astype(jnp.bfloat16)
            for x, c in enumerate(cols):
                o_ref[group, here, c] = out[x * TILE : (x + 1) * TILE]
            dp = matmul(do, v_all[keys], NT)
            delta = jnp.sum(out.astype(jnp.float32) * do.astype(jnp.float32), 1, keepdims=True)
            ds = weight * (dp - delta).astype(jnp.bfloat16)
            tile, first = unit
            ds_ref[group, tile, first * TILE : (first + per_call) * TILE, keys.start - tile * TILE :] = ds
            return ds

        def sums(unit, weight, ds):
            _, keys, _ = places(unit)
            dv_sum[:, keys] += matmul(stacked(do_ref, unit), weight, TN)
            dk_sum[:, keys] += matmul(stacked(q_ref, unit), ds, TN)

        ahead = scores(units[0])
        before = None
        for index, unit in enumerate(units):
            now = ahead
            if index + 1 < len(units):
                ahead = scores(units[index + 1])
            weight = softmax(unit, now).astype(jnp.bfloat16)
            if before is not None:
                sums(*before)
            before = (unit, weight, score_grads(unit, weight))
        sums(*before)
        if lowest:
            for tile in range(tiles):
                gap = max(0, lowest - tile * TILE)
                ds_ref[group, tile, :, :gap] = jnp.zeros((heads * TILE, gap), jnp.bfloat16)

        here = lanes(group)
        own_ref[0, :, here] = dk_sum[:, 2 * rows :].T * FACTOR
        own_ref[1, :, here] = dv_sum[:, 2 * rows :].T
        for place in range(2):
            span = slice(place * rows, (place + 1) * rows)
            back_ref[place, 0, :, here] = (dk_sum[:, span].T * FACTOR).astype(jnp.bfloat16)
            back_ref[place, 1, :, here] = dv_sum[:, span].T.astype(jnp.bfloat16)

    def later(index, carry):
        begin, start = carry
        return begin + first_ref[index + 1], jnp.where(begin <= first_ref[0], begin, start)

    _, start = lax.fori_loop(0, first_ref.shape[0] - 1, later, (jnp.int32(0), jnp.int32(0)))
    reaches_far = start < first_ref[0] - rows

    @pl.when(reaches_far)
    def _():
        all_units(0)

    @pl.when(jnp.logical_not(reaches_far))
    def _():
        all_units(rows)

    @pl.when(group == groups - 1)
    def _():
        for fetch in fetches:
            fetch.wait()


def attention(base, groups, skipped, head_cols, first, bias, q, do, far, near, own, whole_q=None, whole_do=None):
    rows = q.shape[0]
    tiles, _, band = bias.shape
    whole = pl.BlockSpec(memory_space=pltpu.VMEM)
    fetching = whole_q is not None
    far_away = pl.BlockSpec(memory_space=pltpu.HBM)
    rest = (rows, whole_q.shape[1] - q.shape[1] if fetching else 0)
    return pl.pallas_call(
        functools.partial(attention_kernel, base, skipped, fetching),
        grid=(groups,),
        in_specs=[pl.BlockSpec(memory_space=pltpu.SMEM), whole, whole, whole, whole, whole, whole] + [far_away, far_away] * fetching,
        out_specs=[whole] * (6 if fetching else 4),
        out_shape=[
            jax.ShapeDtypeStruct((groups, rows, head_cols), jnp.bfloat16),
            jax.ShapeDtypeStruct((groups, tiles, head_cols // HEAD_DIM * TILE, band), jnp.bfloat16),
            jax.ShapeDtypeStruct((2, 2, rows, groups * HEAD_DIM), jnp.bfloat16),
            jax.ShapeDtypeStruct((2, rows, groups * HEAD_DIM), jnp.float32),
        ]
        + [jax.ShapeDtypeStruct(rest, q.dtype)] * (2 if fetching else 0),
        scratch_shapes=[
            pltpu.VMEM((3 * rows, HEAD_DIM), jnp.bfloat16),
            pltpu.VMEM((3 * rows, HEAD_DIM), jnp.bfloat16),
            pltpu.VMEM((HEAD_DIM, 3 * rows), jnp.float32),
            pltpu.VMEM((HEAD_DIM, 3 * rows), jnp.float32),
        ]
        + [pltpu.SemaphoreType.DMA((2,))] * fetching,
        compiler_params=pltpu.CompilerParams(vmem_limit_bytes=VMEM_LIMIT),
        name="attention",
    )(first, bias, q, do, far, near, own, *((whole_q, whole_do) if fetching else ()))


def query_kernel(calls, skips, *refs):
    o_out, dq_out, k_all, held, sems = refs[-5:]
    rows = held.shape[0]
    wide = held.shape[1] // sum(calls)
    groups = [(index, here) for index, size in enumerate(calls) for here in range(size)]
    copies = []
    for place, (index, here) in enumerate(groups):
        cols = pl.ds(place * wide, wide)
        copies.append(pltpu.make_async_copy(refs[5 * index].at[here], o_out.at[:, cols], sems.at[place, 0]))
        copies[-1].start()
    for place, (index, here) in enumerate(groups):
        _, ds_ref, *parts = refs[5 * index : 5 * index + 5]
        column = slice((skips[index] + here) * HEAD_DIM, (skips[index] + here + 1) * HEAD_DIM)
        for spot, part in enumerate(parts):
            k_all[spot * rows : (spot + 1) * rows] = part[:, column]
        for tile in range(ds_ref.shape[1]):
            k = k_all[tile * TILE : tile * TILE + ds_ref.shape[3]]
            dq = (matmul(ds_ref[here, tile], k, NN) * FACTOR).astype(jnp.bfloat16)
            for x in range(wide // HEAD_DIM):
                start = place * wide + x * HEAD_DIM
                held[tile * TILE : (tile + 1) * TILE, start : start + HEAD_DIM] = dq[x * TILE : (x + 1) * TILE]
        cols = pl.ds(place * wide, wide)
        copies.append(pltpu.make_async_copy(held.at[:, cols], dq_out.at[:, cols], sems.at[place, 1]))
        copies[-1].start()
    for copy in copies:
        copy.wait()


def query_grads(calls, skips, shape, parts):
    rows, width = shape
    flat = [array for part in parts for array in part]
    return pl.pallas_call(
        functools.partial(query_kernel, calls, skips),
        in_specs=[pl.BlockSpec(memory_space=pltpu.VMEM)] * len(flat),
        out_specs=[pl.BlockSpec(memory_space=pltpu.HBM)] * 2,
        out_shape=[jax.ShapeDtypeStruct(shape, jnp.bfloat16)] * 2,
        scratch_shapes=[
            pltpu.VMEM((3 * rows, HEAD_DIM), jnp.bfloat16),
            pltpu.VMEM(shape, jnp.bfloat16),
            pltpu.SemaphoreType.DMA((sum(calls), 2)),
        ],
        compiler_params=pltpu.CompilerParams(vmem_limit_bytes=QUERY_LIMIT),
        name="query_grads",
    )(*flat)


def finish_kernel(base, aliased, *refs):
    refs = refs[2:] if aliased else refs
    kept_ref, returned_ref, gk_ref, gv_ref, total, sems = refs
    span = pl.ds(base * HEAD_DIM, kept_ref.shape[2])
    copies = []
    for index, out in enumerate((gk_ref, gv_ref)):
        total[index] = (kept_ref[index] + returned_ref[index].astype(jnp.float32)).astype(jnp.bfloat16)
        copies.append(pltpu.make_async_copy(total.at[index], out.at[:, span], sems.at[index]))
        copies[-1].start()
    for copy in copies:
        copy.wait()


def finished(base, shape, kept, returned, carried):
    aliased = carried is not None
    carried = carried if aliased else ()
    kept_place = pl.BlockSpec(memory_space=pl.ANY)
    whole = pl.BlockSpec(memory_space=pltpu.VMEM)
    return pl.pallas_call(
        functools.partial(finish_kernel, base, aliased),
        in_specs=[kept_place] * len(carried) + [whole, whole],
        out_specs=[pl.BlockSpec(memory_space=pltpu.HBM)] * 2,
        out_shape=[jax.ShapeDtypeStruct(shape, jnp.bfloat16)] * 2,
        scratch_shapes=[
            pltpu.VMEM((2, shape[0], kept.shape[2]), jnp.bfloat16),
            pltpu.SemaphoreType.DMA((2,)),
        ],
        input_output_aliases={0: 0, 1: 1} if aliased else {},
        compiler_params=pltpu.CompilerParams(vmem_limit_bytes=SMALL_LIMIT),
        name="finish_keys_values",
    )(*carried, kept, returned)


def on_device(queries, keys, values, grad_out, episode_lengths):
    rows = queries.shape[0]
    groups = keys.shape[1] // HEAD_DIM
    count = lax.axis_size("seq")
    place = lax.axis_index("seq").astype(jnp.int32)
    odd = lax.bitwise_and(place, jnp.int32(1))
    first = jnp.reshape(place * rows, (1,))
    ahead = [(source, (source + 2) % count) for source in range(count)]
    behind = [((source + 2) % count, source) for source in range(count)]
    ahead_open = ahead[: count - 2]
    behind_open = behind[: count - 2]
    swap = [(source, source ^ 1) for source in range(count)]
    known = groups == sum(SENT)
    sent = SENT if known else (groups,)
    calls = CALLS if known else (groups,)
    returns = RETURNED if known else (groups,)
    starts = [sum(sent[:index]) for index in range(len(sent))]

    q_here, do_here, k_here, v_here = (in_hbm(x) for x in (queries, grad_out, keys, values))
    own = list(packed(k_here, v_here, [start * HEAD_DIM for start in starts], [size * HEAD_DIM for size in sent]))
    far = [permuted(block, ahead_open if index else ahead) for index, block in enumerate(own)]
    head_cols = queries.shape[1] // groups
    begins = jnp.concatenate([first, episode_lengths])
    bias, q_part, do_part = prepared(episode_lengths, first, q_here, do_here, calls[0] * head_cols)
    own[0], bias = lax.optimization_barrier((own[0], bias))
    near = []
    grads = None
    parts = []
    waiting = []
    stored = []
    skips = []
    base = begun = 0
    for size in calls:
        chunk = max(index for index, start in enumerate(starts) if start <= base)
        skips.append(base - starts[chunk])
        if chunk == len(near):
            there = far[chunk]
            if stored:
                there, ds = lax.optimization_barrier((there, stored[-1][1]))
                stored[-1] = (stored[-1][0], ds) + stored[-1][2:]
            near.append(permuted(jnp.where(odd == 1, there, own[chunk]), swap))
        if base == 0 and size < groups:
            out, ds, back, kept, q_part, do_part = attention(
                0, size, skips[-1], head_cols, begins, bias, q_part, do_part, far[chunk], near[chunk], own[chunk], q_here, do_here
            )
        else:
            out, ds, back, kept = attention(
                base - (calls[0] if base else 0), size, skips[-1], head_cols, begins, bias, q_part, do_part, far[chunk], near[chunk], own[chunk]
            )
        stored.append((out, ds, far[chunk], near[chunk], own[chunk]))
        waiting.append((back, kept))
        base += size
        if base < begun + returns[len(parts)]:
            continue
        back = jnp.concatenate([pair[0] for pair in waiting], axis=3)
        kept = jnp.concatenate([pair[1] for pair in waiting], axis=2)
        waiting = []
        if parts:
            back, parts[-1][2] = lax.optimization_barrier((back, parts[-1][2]))
        beside = permuted(back[1], swap)
        none = jnp.zeros_like(beside)
        onward = back[0].astype(jnp.float32) + jnp.where(odd == 1, beside, none).astype(jnp.float32)
        kept = kept + jnp.where(odd == 1, none, beside).astype(jnp.float32)
        parts.append([begun, kept, permuted(onward.astype(jnp.bfloat16), behind_open if parts else behind)])
        begun = base
    attn_out, grad_queries = query_grads(calls, skips, queries.shape, stored)
    for begun, kept, returned in parts:
        grads = finished(begun, keys.shape, kept, returned, grads)
    return (attn_out, grad_queries, *grads)


def solution(mesh):
    split = P(("groups", "seq"), None)
    return jax.shard_map(
        on_device,
        mesh=mesh,
        in_specs=(split, split, split, split, P("groups")),
        out_specs=(split, split, split, split),
        check_vma=False,
    )
```
